128 devices in a mesh: dp: 16 (over x, y), tensor: 8 (over z, core).
Axes of the slice: x: 4, y: 4, z: 4, core: 2. Of those that a mesh axis runs over, the one named last changes fastest.
Arguments:
- query: bfloat16 [16384, 2048], P('dp', 'tensor'), may hold values from -26.25 to 26.25
- key: bfloat16 [16384, 512], P('dp'), may hold values from -26.25 to 26.25
- value: bfloat16 [16384, 512], P('dp'), may hold values from -6 to 6
- grad_out: bfloat16 [16384, 3584], P('dp'), may hold values from -12 to 12
- out_weight: bfloat16 [3584, 2048], P(None, 'tensor'), may hold values from -0.125 to 0.125
- plan: int32 [128], replicated, may hold values from 0 to 127, as said below
- segments: int32 [16384], P('dp'), may hold values from 0 to 1023, as said below
Outputs:
- grad_query: bfloat16 [16384, 2048], P('dp', 'tensor')
- grad_key: bfloat16 [16384, 512], P('dp')
- grad_value: bfloat16 [16384, 512], P('dp')
- grad_out_weight: float32 [3584, 2048], P('dp', 'tensor')
The draws below stay inside these ranges and needn't reach their ends.
Inputs may be any that keep to these rules, and one draw needn't show every extreme that they name: plan is a permutation of the blocks; the 8 blocks that one index of dp holds go to 8 different indices of dp, at most one to each. `segments`: within each aligned block of 1024 rows of one index of dp the ids start at 0 and never fall; ids may skip values.
All inputs are finite; a program needn't handle non-finite values.
Results may differ from the reference program's by a relative error of at most 0.034.
The reference program's roundings to bfloat16 on the way count: a program that leaves them out, or rounds other values in their place, can miss the bound.
Values may be sent and summed in bfloat16 or wider, within the bound.
A program may use at most 128 MiB of HBM per device.

```python
import math
import jax
import jax.numpy as jnp
from jax import lax

D = 3584
KV = 4
HD = 128
HEADS = 16
ROWBLK = 128
TOK_DEV = 1024
HEADS_DEV = 2
BLK_DEV = 8
BLOCKS = 128
TOKENS = 16384
REPLICAS = 16
N_DP = 16


def drawn_pair(key):
    base = jax.random.fold_in(key, 7001)
    subkeys = jax.random.split(base, 2)
    group = HEADS // KV
    key_rows = jnp.clip(jax.random.normal(subkeys[0], (TOKENS, KV, HD), jnp.float32), -5.0, 5.0)
    query_rows = jnp.clip(jax.random.normal(subkeys[1], (TOKENS, KV, group, HD), jnp.float32), -5.0, 5.0)
    return (query_rows.reshape(TOKENS, HEADS * HD), key_rows.reshape(TOKENS, KV * HD))


def draw_query(key, part):
    return drawn_pair(key)[0].astype(jnp.bfloat16)


def draw_key(key, part):
    return drawn_pair(key)[1].astype(jnp.bfloat16)


def draw_segments(key, part):
    base = jax.random.fold_in(key, 5003)
    subkeys = jax.random.split(base, 3)
    spacing = jnp.array([24, 96, 384, 1536, 1000000], dtype=jnp.int32)
    picked = jax.random.randint(subkeys[0], (REPLICAS, 1), 0, 5)
    row_limit = jnp.take(spacing, picked)
    rolled = jax.random.randint(subkeys[1], (REPLICAS, TOK_DEV), 0, 1000000)
    boundary = rolled % row_limit == 0
    boundary = boundary.at[:, 0].set(False)
    marked = jax.random.randint(subkeys[2], (), 0, REPLICAS)
    replica_index = jnp.arange(REPLICAS, dtype=jnp.int32)[:, None]
    row_index = jnp.arange(TOK_DEV, dtype=jnp.int32)[None, :]
    forced = (replica_index == marked) & (row_index == TOK_DEV // 2)
    boundary = boundary | forced
    counted = jnp.cumsum(boundary.astype(jnp.int32), axis=1).astype(jnp.int32)
    last_id = counted[:, -1:]
    lifted = (replica_index == marked) & (counted == last_id)
    return jnp.where(lifted, TOK_DEV - 1, counted).astype(jnp.int32).reshape(TOKENS)


def draw_plan(key, part):
    base = jax.random.fold_in(key, 9001)
    subkeys = jax.random.split(base, 5)
    outer_perm = jax.random.permutation(subkeys[0], REPLICAS)
    rounds = jax.random.permutation(subkeys[1], REPLICAS)[:BLK_DEV]
    inner_perm = jax.random.permutation(subkeys[2], REPLICAS)
    local_order = jax.vmap(lambda subkey: jax.random.permutation(subkey, BLK_DEV))(jax.random.split(subkeys[3], REPLICAS))
    slot_order = jax.vmap(lambda subkey: jax.random.permutation(subkey, BLK_DEV))(jax.random.split(subkeys[4], REPLICAS))
    sender = jnp.arange(REPLICAS)[:, None]
    round_index = jnp.arange(BLK_DEV)[None, :]
    target = outer_perm[(rounds[round_index] + inner_perm[sender]) % REPLICAS]
    target_slot = slot_order[target, round_index]
    destination = (target * BLK_DEV + target_slot).reshape(-1)
    from_block = (sender * BLK_DEV + local_order).reshape(-1)
    return jnp.zeros((BLOCKS,), jnp.int32).at[destination].set(from_block.astype(jnp.int32))


def with_spikes(entries, stream_key, source, target, blocks, factor):
    def block_of(position):
        return (jnp.arange(entries.shape[position]) // (entries.shape[position] // blocks)).reshape((-1,) + (1,) * (entries.ndim - 1 - position))

    one_side = jax.random.permutation(stream_key, blocks)[block_of(target)]
    far = (block_of(target) + blocks // 2) % blocks
    return jnp.where((block_of(source) == one_side) | (block_of(source) == far), factor * entries, entries)


def levels(key, extent, pieces, low, largest):
    factor_of, own = 1.0, jax.random.fold_in(key, 6)
    for dim, parts in pieces:
        draws = jnp.exp(jax.random.uniform(jax.random.fold_in(own, dim), (parts,), jnp.float32, low / len(pieces), largest / len(pieces)))
        factor_of = factor_of * jnp.repeat(draws, extent[dim] // parts).reshape([-1 if axis == dim else 1 for axis in range(len(extent))])
    return factor_of


def scatter_about(key, extent, spread, bound, pieces=(), kind=jnp.bfloat16):
    gain = levels(key, extent, pieces, -0.22, 0.18) if pieces else 1.0
    values = jax.random.normal(key, extent, jnp.float32) * spread * gain
    return jnp.minimum(jnp.maximum(values, -bound), bound).astype(kind)


def heavy_noise(stream_key, shape, deviation, limit, shards, heavy, kind=jnp.bfloat16):
    entries = deviation * jax.random.normal(stream_key, shape, jnp.float32)
    if shards:
        entries = entries * levels(stream_key, shape, shards, -0.22, 0.18)
    return jnp.clip(with_spikes(entries, jax.random.fold_in(stream_key, 3), *heavy), -limit, limit).astype(kind)


def setup_inputs(seed: int = 0) -> dict:
    arg_keys = jax.random.split(jax.random.key(seed), 8)
    query = draw_query(jax.random.fold_in(arg_keys[7], 71), 0)
    key = draw_key(jax.random.fold_in(arg_keys[7], 71), 0)
    value = scatter_about(arg_keys[2], (TOKENS, KV * HD), 1.0, 6.0, ((0, 16),))
    grad_out = heavy_noise(arg_keys[3], (TOKENS, D), 2.0, 12.0, ((0, 16),), (0, 1, 16, 2.0))
    out_weight = scatter_about(arg_keys[4], (D, HEADS * HD), (HEADS * HD) ** -0.5, 0.125, ((1, 8),))
    plan = draw_plan(jax.random.fold_in(arg_keys[7], 71), 0)
    segments = draw_segments(jax.random.fold_in(arg_keys[7], 71), 0)
    return {"query": query, "key": key, "value": value, "grad_out": grad_out, "out_weight": out_weight, "plan": plan, "segments": segments}


rope_base = 1000000.0
yarn_factor = 4.0
yarn_context = 32768.0
beta_fast = 32.0
beta_slow = 1.0
masked_score = -1e+30

def yarn_frequencies(head_size):
    half_size = head_size // 2

    def correction(rotations):
        return head_size * math.log(yarn_context / (rotations * 2.0 * math.pi)) / (2.0 * math.log(rope_base))
    lower_bound = max(math.floor(correction(beta_fast)), 0)
    upper_bound = min(math.ceil(correction(beta_slow)), head_size - 1)
    ramp_span = max(upper_bound - lower_bound, 0.001)
    row_index = jnp.arange(half_size).astype(jnp.float32)
    extrap_freq = rope_base ** (-2.0 * row_index / head_size)
    interp_freq = extrap_freq / yarn_factor
    ramp_weight = jnp.clip((row_index - lower_bound) / ramp_span, 0.0, 1.0)
    return interp_freq * ramp_weight + extrap_freq * (1.0 - ramp_weight)

def positions_of(segments):
    row_count = segments.shape[-1]
    row_index = jnp.arange(row_count, dtype=jnp.int32)
    is_start = jnp.concatenate([jnp.ones(segments.shape[:-1] + (1,), dtype=jnp.bool_), segments[..., 1:] != segments[..., :-1]], axis=-1)
    seg_start = lax.cummax(jnp.where(is_start, row_index, 0).astype(jnp.int32), axis=segments.ndim - 1)
    return row_index - seg_start

def rotate(values, cosine, sine):
    half_size = values.shape[-1] // 2
    first_half = values[..., :half_size]
    second_half = values[..., half_size:]
    return jnp.concatenate([first_half * cosine - second_half * sine, second_half * cosine + first_half * sine], axis=-1)

def unrotate(grads, cosine, sine):
    half_size = grads.shape[-1] // 2
    first_half = grads[..., :half_size]
    second_half = grads[..., half_size:]
    return jnp.concatenate([first_half * cosine + second_half * sine, second_half * cosine - first_half * sine], axis=-1)

def reference(query, key, value, grad_out, out_weight, plan, segments):
    group = HEADS // KV
    inv_scale = 1.0 / math.sqrt(HD)
    factor = 0.1 * math.log(yarn_factor) + 1.0

    def to_dest(array):
        blocked = array.reshape((BLOCKS, ROWBLK) + array.shape[1:])
        return jnp.take(blocked, plan, axis=0).reshape(array.shape)

    def to_source(array):
        blocked = array.reshape((BLOCKS, ROWBLK) + array.shape[1:])
        return jnp.zeros_like(blocked).at[plan].set(blocked).reshape(array.shape)
    moved_query = to_dest(query)
    moved_key = to_dest(key)
    moved_value = to_dest(value)
    moved_grad = to_dest(grad_out)
    places = positions_of(segments.reshape(N_DP, TOK_DEV)).reshape(TOKENS)
    angles = places.astype(jnp.float32)[:, None] * yarn_frequencies(HD)[None, :]
    cosine = jnp.cos(angles) * factor
    sine = jnp.sin(angles) * factor
    rot_query = rotate(moved_query.astype(jnp.float32).reshape(TOKENS, HEADS, HD), cosine[:, None, :], sine[:, None, :]).astype(jnp.bfloat16)
    rot_key = rotate(moved_key.astype(jnp.float32).reshape(TOKENS, KV, HD), cosine[:, None, :], sine[:, None, :]).astype(jnp.bfloat16)
    grad_attn = jnp.dot(moved_grad, out_weight, preferred_element_type=jnp.float32).astype(jnp.bfloat16)
    row_index = jnp.arange(TOK_DEV, dtype=jnp.int32)
    causal = row_index[None, :] <= row_index[:, None]

    def one_replica(items):
        query_rows, key_rows, value_rows, grad_rows, seg_rows = items
        query_f = query_rows.astype(jnp.float32)
        key_f = jnp.repeat(key_rows.astype(jnp.float32), group, axis=1)
        value_f = jnp.repeat(value_rows.astype(jnp.float32), group, axis=1)
        grad_f = grad_rows.astype(jnp.float32).reshape(TOK_DEV, HEADS, HD)
        allowed = (seg_rows[:, None] == seg_rows[None, :]) & causal
        scores = jnp.einsum('qhd,khd->hqk', query_f, key_f) * inv_scale
        scores = jnp.where(allowed[None], scores, masked_score)
        row_peak = lax.optimization_barrier(jnp.max(scores, axis=2, keepdims=True))
        exp_scores = jnp.exp(scores - row_peak)
        prob_full = exp_scores / lax.optimization_barrier(jnp.sum(exp_scores, axis=2, keepdims=True))
        prob_bf = lax.optimization_barrier(prob_full.astype(jnp.bfloat16))
        prob_f = prob_bf.astype(jnp.float32)
        head_out = jnp.einsum('hqk,khd->qhd', prob_f, value_f).astype(jnp.bfloat16)
        grad_prob = jnp.einsum('qhd,khd->hqk', grad_f, value_f)
        row_delta = lax.optimization_barrier(jnp.sum(grad_f * head_out.astype(jnp.float32), axis=2))
        grad_bf = lax.optimization_barrier((prob_full * (grad_prob - jnp.transpose(row_delta)[:, :, None])).astype(jnp.bfloat16))
        grad_score = grad_bf.astype(jnp.float32)
        grad_rot_query = jnp.einsum('hqk,khd->qhd', grad_score, key_f) * inv_scale
        grad_rot_key = jnp.einsum('hqk,qhd->khd', grad_score, query_f) * inv_scale
        grad_value_heads = jnp.einsum('hqk,qhd->khd', prob_f, grad_f)
        return (head_out, grad_rot_query, grad_rot_key, grad_value_heads)
    stacked = (rot_query.reshape(N_DP, TOK_DEV, HEADS, HD), rot_key.reshape(N_DP, TOK_DEV, KV, HD), moved_value.reshape(N_DP, TOK_DEV, KV, HD), grad_attn.reshape(N_DP, TOK_DEV, HEADS * HD), segments.reshape(N_DP, TOK_DEV))
    head_out, grad_rot_query, grad_rot_key, grad_value_heads = lax.map(one_replica, stacked)
    head_out = head_out.reshape(TOKENS, HEADS * HD)
    grad_query = unrotate(grad_rot_query.reshape(TOKENS, HEADS, HD), cosine[:, None, :], sine[:, None, :]).astype(jnp.bfloat16).reshape(TOKENS, HEADS * HD)
    head_runs = HEADS // HEADS_DEV
    key_sum = grad_rot_key.reshape(TOKENS, head_runs, HEADS_DEV, HD).sum(axis=2)
    key_partial = lax.optimization_barrier(unrotate(key_sum, cosine[:, None, :], sine[:, None, :]).astype(jnp.bfloat16))
    value_partial = lax.optimization_barrier(grad_value_heads.reshape(TOKENS, head_runs, HEADS_DEV, HD).sum(axis=2).astype(jnp.bfloat16))
    runs_per_key = group // HEADS_DEV
    grad_key = key_partial.astype(jnp.float32).reshape(TOKENS, KV, runs_per_key, HD).sum(axis=2).astype(jnp.bfloat16).reshape(TOKENS, KV * HD)
    grad_value = value_partial.astype(jnp.float32).reshape(TOKENS, KV, runs_per_key, HD).sum(axis=2).astype(jnp.bfloat16).reshape(TOKENS, KV * HD)
    grad_out_weight = jnp.dot(moved_grad.T, head_out, preferred_element_type=jnp.float32) * (1.0 / N_DP)
    return (to_source(grad_query), to_source(grad_key), to_source(grad_value), grad_out_weight)
```

```python
from functools import partial
import math

import jax
import jax.numpy as jnp
from jax import lax
from jax.sharding import PartitionSpec as P

KV = 4
HD = 128
HEADS = 16
ROWBLK = 128


rope_base = 1000000.0
yarn_factor = 4.0
yarn_context = 32768.0
beta_fast = 32.0
beta_slow = 1.0
masked_score = -1e30


def yarn_frequencies(head_size):
    half_size = head_size // 2

    def correction(rotations):
        return (
            head_size
            * math.log(yarn_context / (rotations * 2.0 * math.pi))
            / (2.0 * math.log(rope_base))
        )

    lower_bound = max(math.floor(correction(beta_fast)), 0)
    upper_bound = min(math.ceil(correction(beta_slow)), head_size - 1)
    ramp_span = max(upper_bound - lower_bound, 0.001)
    row_index = jnp.arange(half_size).astype(jnp.float32)
    extrap_freq = rope_base ** (-2.0 * row_index / head_size)
    interp_freq = extrap_freq / yarn_factor
    ramp_weight = jnp.clip((row_index - lower_bound) / ramp_span, 0.0, 1.0)
    return interp_freq * ramp_weight + extrap_freq * (1.0 - ramp_weight)


def positions_of(segments):
    row_index = jnp.arange(segments.shape[0], dtype=jnp.int32)
    smaller = segments[None, :] < segments[:, None]
    return row_index - jnp.sum(smaller.astype(jnp.int32), axis=1)


def rotate(values, cosine, sine):
    half_size = values.shape[-1] // 2
    first_half = values[..., :half_size]
    second_half = values[..., half_size:]
    return jnp.concatenate(
        [first_half * cosine - second_half * sine, second_half * cosine + first_half * sine],
        axis=-1,
    )


def unrotate(grads, cosine, sine):
    half_size = grads.shape[-1] // 2
    first_half = grads[..., :half_size]
    second_half = grads[..., half_size:]
    return jnp.concatenate(
        [first_half * cosine + second_half * sine, second_half * cosine - first_half * sine],
        axis=-1,
    )


def rope_tables(segments, head_size):
    places = positions_of(segments)
    angles = places.astype(jnp.float32)[:, None] * yarn_frequencies(head_size)[None, :]
    factor = 0.1 * math.log(yarn_factor) + 1.0
    return (jnp.cos(angles) * factor, jnp.sin(angles) * factor)


def pick(blocks, slots):
    return jnp.concatenate(
        [lax.dynamic_slice_in_dim(blocks, slots[i], 1, 0) for i in range(slots.shape[0])]
    )


def pack_blocks(blocks, slots):
    return pick(blocks, slots)


def score_tile(stacked, key_tile, key_seg, key_pos, query_seg, query_pos, inv_scale):
    raw_scores = jnp.dot(stacked, key_tile.T, preferred_element_type=jnp.float32) * inv_scale
    allowed = (query_seg[:, None] == key_seg[None, :]) & (key_pos[None, :] <= query_pos[:, None])
    return jnp.where(allowed, raw_scores, masked_score)


def attend(queries, key_rows, value_rows, upstream, segments):
    head_count, row_count, head_size = queries.shape
    tile_rows = min(512, row_count)
    tile_count = row_count // tile_rows
    inv_scale = 1.0 / math.sqrt(head_size)
    row_index = jnp.arange(row_count, dtype=jnp.int32)
    stacked_rows = head_count * tile_rows
    key_grads = [jnp.zeros((tile_rows, head_size), jnp.float32) for unused in range(tile_count)]
    value_grads = [jnp.zeros((tile_rows, head_size), jnp.float32) for unused in range(tile_count)]
    query_grads = []
    outputs = []
    for query_block in range(tile_count):
        row_start = query_block * tile_rows
        stacked = queries[:, row_start : row_start + tile_rows].reshape(stacked_rows, head_size)
        incoming = upstream[:, row_start : row_start + tile_rows].reshape(stacked_rows, head_size)
        query_seg = jnp.tile(segments[row_start : row_start + tile_rows], head_count)
        query_pos = jnp.tile(row_index[row_start : row_start + tile_rows], head_count)
        tile_list = list(range(tile_count))
        tile_flags = []
        for key_block in tile_list:
            tile_flags.append(None)
        score_tiles = []
        for key_block, tile_flag in zip(tile_list, tile_flags):
            key_start = key_block * tile_rows
            compute = partial(
                score_tile,
                stacked,
                key_rows[key_start : key_start + tile_rows],
                segments[key_start : key_start + tile_rows],
                row_index[key_start : key_start + tile_rows],
                query_seg,
                query_pos,
                inv_scale,
            )
            score_tiles.append(compute())
        scores = jnp.concatenate(score_tiles, axis=1)
        row_peak = jnp.max(scores, axis=1, keepdims=True)
        exp_scores = jnp.exp(scores - row_peak)
        prob_full = exp_scores / jnp.sum(exp_scores, axis=1, keepdims=True)
        prob_bf = prob_full.astype(jnp.bfloat16)
        head_out = jnp.zeros((stacked_rows, head_size), jnp.float32)
        for key_block, tile_flag in zip(tile_list, tile_flags):
            key_start = key_block * tile_rows
            compute = partial(
                jnp.dot,
                prob_bf[:, key_start : key_start + tile_rows],
                value_rows[key_start : key_start + tile_rows],
                preferred_element_type=jnp.float32,
            )
            head_out = head_out + compute()
        out_bf = head_out.astype(jnp.bfloat16)
        row_delta = jnp.sum(
            incoming.astype(jnp.float32) * out_bf.astype(jnp.float32), axis=1, keepdims=True
        )
        grad_tiles = []
        for key_block, tile_flag in zip(tile_list, tile_flags):
            key_start = key_block * tile_rows
            compute = partial(
                jnp.dot,
                incoming,
                value_rows[key_start : key_start + tile_rows].T,
                preferred_element_type=jnp.float32,
            )
            grad_tiles.append(compute())
        grad_prob = jnp.concatenate(grad_tiles, axis=1)
        grad_score = (prob_full * (grad_prob - row_delta)).astype(jnp.bfloat16)
        query_grad = jnp.zeros((stacked_rows, head_size), jnp.float32)
        for key_block, tile_flag in zip(tile_list, tile_flags):
            key_start = key_block * tile_rows
            score_piece = grad_score[:, key_start : key_start + tile_rows]
            prob_piece = prob_bf[:, key_start : key_start + tile_rows]
            query_grad = (
                query_grad
                + partial(
                    jnp.dot,
                    score_piece,
                    key_rows[key_start : key_start + tile_rows],
                    preferred_element_type=jnp.float32,
                )()
            )
            key_grads[key_block] = (
                key_grads[key_block]
                + partial(jnp.dot, score_piece.T, stacked, preferred_element_type=jnp.float32)()
            )
            value_grads[key_block] = (
                value_grads[key_block]
                + partial(jnp.dot, prob_piece.T, incoming, preferred_element_type=jnp.float32)()
            )
        query_grads.append((query_grad * inv_scale).reshape(head_count, tile_rows, head_size))
        outputs.append(out_bf.reshape(head_count, tile_rows, head_size))
    key_total = jnp.concatenate(key_grads, axis=0) * inv_scale
    value_total = jnp.concatenate(value_grads, axis=0)
    return (
        jnp.concatenate(query_grads, axis=1),
        jnp.concatenate(outputs, axis=1),
        key_total,
        value_total,
    )


def weight_term(grad_rows, attn_rows):
    term = jnp.dot(grad_rows.T, attn_rows, preferred_element_type=jnp.float32)
    ranks = lax.axis_size("dp")
    pieces = term.astype(jnp.bfloat16).reshape(ranks, term.shape[0] // ranks, term.shape[1])
    arrived = lax.all_to_all(pieces, "dp", split_axis=0, concat_axis=0, tiled=True)
    return jnp.sum(arrived.astype(jnp.float32), axis=0)


def local(query, key, value, grad_out, out_weight, plan, segments):
    rank_count = lax.axis_size("dp")
    lane_count = lax.axis_size("tensor")
    my_rank = lax.axis_index("dp")
    my_lane = lax.axis_index("tensor")
    row_count = query.shape[0]
    block_count = row_count // ROWBLK
    head_size = HD
    local_heads = query.shape[1] // head_size
    group = HEADS // KV
    kv_head = my_lane * local_heads // group
    own_key = lax.dynamic_slice_in_dim(key, kv_head * head_size, head_size, 1)
    own_value = lax.dynamic_slice_in_dim(value, kv_head * head_size, head_size, 1)
    plan_table = plan.reshape(rank_count, block_count)
    source_rank = plan_table // block_count
    source_slot = plan_table % block_count
    from_mine = source_rank == my_rank
    send_slot = jnp.sum(jnp.where(from_mine, source_slot, 0), axis=1)
    arrive_from = lax.dynamic_index_in_dim(source_rank, my_rank, 0, keepdims=False)
    senders = jnp.arange(rank_count, dtype=jnp.int32)
    slot_match = arrive_from[None, :] == senders[:, None]
    back_slot = jnp.sum(
        jnp.where(slot_match, jnp.arange(block_count, dtype=jnp.int32)[None, :], 0), axis=1
    )
    landing = from_mine[:, :, None] & (
        source_slot[:, :, None] == jnp.arange(block_count, dtype=jnp.int32)[None, None, :]
    )
    return_rank = jnp.sum(jnp.where(landing, senders[:, None, None], 0), axis=(0, 1))

    def outbound(array):
        return pack_blocks(
            array.reshape((block_count, ROWBLK, array.shape[1])), send_slot
        )

    def inbound(received):
        return pick(received, arrive_from).reshape(row_count, received.shape[2])

    def homeward(array):
        return pack_blocks(
            array.reshape((block_count, ROWBLK, array.shape[1])), back_slot
        )

    def landed(received):
        return pick(received, return_rank).reshape(row_count, received.shape[2])

    source_grad = jnp.dot(grad_out, out_weight, preferred_element_type=jnp.float32).astype(
        jnp.bfloat16
    )
    columns = local_heads * head_size
    packed = outbound(jnp.concatenate([query, source_grad, own_key, own_value], axis=1))
    moved = inbound(lax.all_to_all(packed, "dp", split_axis=0, concat_axis=0, tiled=True))
    query_dest = moved[:, :columns]
    attn_grad = moved[:, columns : 2 * columns]
    key_dest = moved[:, 2 * columns : 2 * columns + head_size]
    value_dest = moved[:, 2 * columns + head_size :]
    cosine, sine = rope_tables(segments, head_size)
    rot_query = rotate(
        query_dest.reshape(row_count, local_heads, head_size).astype(jnp.float32),
        cosine[:, None, :],
        sine[:, None, :],
    ).astype(jnp.bfloat16)
    rot_key = rotate(key_dest.astype(jnp.float32), cosine, sine).astype(jnp.bfloat16)
    query_heads = jnp.transpose(rot_query, (1, 0, 2))
    upstream_heads = jnp.transpose(attn_grad.reshape(row_count, local_heads, head_size), (1, 0, 2))
    query_grad, outputs, key_grad, value_grad = attend(
        query_heads, rot_key, value_dest, upstream_heads, segments
    )
    grad_rows_query = (
        unrotate(jnp.transpose(query_grad, (1, 0, 2)), cosine[:, None, :], sine[:, None, :])
        .astype(jnp.bfloat16)
        .reshape(row_count, local_heads * head_size)
    )
    key_partial = unrotate(key_grad, cosine, sine).astype(jnp.bfloat16)
    value_partial = value_grad.astype(jnp.bfloat16)
    attn_out = jnp.transpose(outputs, (1, 0, 2)).reshape(row_count, local_heads * head_size)
    packed = homeward(
        jnp.concatenate([attn_out, grad_rows_query, key_partial, value_partial], axis=1)
    )
    returned = landed(lax.all_to_all(packed, "dp", split_axis=0, concat_axis=0, tiled=True))
    attn_source = returned[:, :columns]
    grad_query = returned[:, columns : 2 * columns]
    key_source = returned[:, 2 * columns : 2 * columns + head_size]
    value_source = returned[:, 2 * columns + head_size :]
    weight_grad = weight_term(grad_out, attn_source)
    key_all, value_all = (
        lax.all_gather(key_source, "tensor", axis=1, tiled=True),
        lax.all_gather(value_source, "tensor", axis=1, tiled=True),
    )
    lanes_per_key = group // local_heads

    def combine(gathered):
        merged = (
            gathered.astype(jnp.float32)
            .reshape(row_count, KV, lanes_per_key, head_size)
            .sum(axis=2)
        )
        return merged.astype(jnp.bfloat16).reshape(row_count, KV * head_size)

    return (grad_query, combine(key_all), combine(value_all), weight_grad * (1.0 / rank_count))


def solution(mesh):
    in_specs = (
        P("dp", "tensor"),
        P("dp", None),
        P("dp", None),
        P("dp", None),
        P(None, "tensor"),
        P(),
        P("dp"),
    )
    out_specs = (P("dp", "tensor"), P("dp", None), P("dp", None), P("dp", "tensor"))
    return jax.shard_map(local, mesh=mesh, in_specs=in_specs, out_specs=out_specs, check_vma=False)
```

```python
import functools
import math

import jax
import jax.numpy as jnp
from jax import lax
from jax.experimental import pallas as pl
from jax.experimental.pallas import tpu as pltpu
from jax.sharding import PartitionSpec as P

D = 3584
KV = 4
HD = 128
HEADS = 16
RB = 128
NB = 8
RANKS = 16
LANES = 8
COLS = 256
TILE = 256
TILES = NB * RB // TILE
WROWS = D // RANKS

rope_base = 1000000.0
yarn_factor = 4.0
yarn_context = 32768.0
beta_fast = 32.0
beta_slow = 1.0
masked_score = -1e30
MESH = pl.DeviceIdType.MESH
BF = jnp.bfloat16
F32 = jnp.float32


def yarn_frequencies(head_size):
    half_size = head_size // 2

    def correction(rotations):
        return (
            head_size
            * math.log(yarn_context / (rotations * 2.0 * math.pi))
            / (2.0 * math.log(rope_base))
        )

    lower_bound = max(math.floor(correction(beta_fast)), 0)
    upper_bound = min(math.ceil(correction(beta_slow)), head_size - 1)
    ramp_span = max(upper_bound - lower_bound, 0.001)
    row_index = jnp.arange(half_size).astype(jnp.float32)
    extrap_freq = rope_base ** (-2.0 * row_index / head_size)
    interp_freq = extrap_freq / yarn_factor
    ramp_weight = jnp.clip((row_index - lower_bound) / ramp_span, 0.0, 1.0)
    return interp_freq * ramp_weight + extrap_freq * (1.0 - ramp_weight)


def dot(a, b, dims):
    return lax.dot_general(a, b, (dims, ((), ())), preferred_element_type=F32)


NN = ((1,), (0,))
NT = ((1,), (1,))
TN = ((0,), (0,))


def kernel(
    plan, seg, freq, q_hbm, k_hbm, v_hbm, g_hbm, w_hbm,
    gq_hbm, gk_hbm, gv_hbm, gw_hbm,
    q_v, kv_v, g_v, w_v, qkv_s, qkv_r, ga_v, ga_s, ga_r, kv2, qs, gas, outs, prob,
    ao_s, ao_r, dq_v, dq_s, dq_r, dkt, dvt, dkv_own, dkv_in, dkv_v, dkv_s, dkv_r,
    w_s, w_r, zk, aoh, gw_v, cosf, sinf, start,
    in_sem, g_sem, send_sem, recv_sem, pair_send, pair_recv, z_send, z_recv, out_sem,
):
    me = lax.axis_index("dp")
    lane = lax.axis_index("tensor")
    core = lax.rem(lane, 2)
    zed = lane // 2
    partner = lane + 1 - 2 * core
    inv_scale = 1.0 / math.sqrt(HD)
    log2_scale = inv_scale * math.log2(math.e)

    q_in = pltpu.make_async_copy(q_hbm, q_v, in_sem.at[0])
    q_in.start()
    head_cols = pl.ds(pl.multiple_of(zed * HD, HD), HD)
    k_in = pltpu.make_async_copy(k_hbm.at[:, :, head_cols], kv_v, in_sem.at[1])
    v_in = pltpu.make_async_copy(v_hbm.at[:, :, head_cols], kv_v, in_sem.at[1])
    pl.when(core == 0)(k_in.start)
    pl.when(core == 1)(v_in.start)
    w_in = pltpu.make_async_copy(w_hbm, w_v, in_sem.at[2])
    w_in.start()
    g_in = [
        pltpu.make_async_copy(
            g_hbm.at[pl.ds(2 * t, 2)], g_v.at[pl.ds(2 * t, 2)], g_sem.at[t]
        )
        for t in range(TILES)
    ]
    for copy in g_in:
        copy.start()

    barrier = pltpu.get_barrier_semaphore()

    def greet(o, carry):
        pl.semaphore_signal(
            barrier, inc=1, device_id={"dp": lax.rem(me + o, RANKS)}, device_id_type=MESH
        )
        return carry

    lax.fori_loop(1, RANKS, greet, 0)
    pl.semaphore_signal(barrier, inc=1, device_id={"tensor": partner}, device_id_type=MESH)
    for o in range(1, 4):
        peer = lax.rem(zed + o, 4) * 2 + core
        pl.semaphore_signal(barrier, inc=1, device_id={"tensor": peer}, device_id_type=MESH)

    def send_slot(dest):
        slot = jnp.int32(0)
        for b in range(NB):
            source = plan[dest * NB + b]
            slot = jnp.where((source >> 3) == me, source & 7, slot)
        return slot

    def back_slot(dest):
        slot = jnp.int32(0)
        for b in range(NB):
            slot = jnp.where((plan[me * NB + b] >> 3) == dest, b, slot)
        return slot

    def moved(stage, landing, kind, dest):
        return pltpu.make_async_remote_copy(
            src_ref=stage.at[dest],
            dst_ref=landing.at[me],
            send_sem=send_sem.at[kind],
            recv_sem=recv_sem.at[kind],
            device_id={"dp": dest},
            device_id_type=MESH,
        )

    def all_moved(stage, landing, kind):
        rest = pl.ds(0, RANKS - 1)
        return pltpu.make_async_remote_copy(
            src_ref=stage.at[rest],
            dst_ref=landing.at[rest],
            send_sem=send_sem.at[kind],
            recv_sem=recv_sem.at[kind],
            device_id={"dp": lax.rem(me + 1, RANKS)},
            device_id_type=MESH,
        )

    def exchange(fill, stage, landing, kind):
        def one(o, carry):
            dest = lax.rem(me + o, RANKS)
            fill(stage, dest, dest)
            moved(stage, landing, kind, dest).start()
            return carry

        lax.fori_loop(1, RANKS, one, 0)
        fill(landing, me, me)

    q_in.wait()
    pl.when(core == 0)(k_in.wait)
    pl.when(core == 1)(v_in.wait)
    pl.semaphore_wait(barrier, RANKS - 1 + 4)

    def fill_qkv(buffer, at, dest):
        slot = send_slot(dest)
        buffer[at, :, :COLS] = q_v[slot]
        buffer[at, :, COLS:] = kv_v[slot]

    exchange(fill_qkv, qkv_s, qkv_r, 0)

    w_in.wait()
    for t in range(TILES):
        g_in[t].wait()
    def project(t, carry):
        rows = pl.ds(2 * t, 2)
        product = dot(g_v[rows].reshape(TILE, D), w_v[...], NN)
        ga_v[rows] = product.astype(BF).reshape(2, RB, COLS)
        return carry

    lax.fori_loop(0, TILES, project, 0)

    def fill_ga(buffer, at, dest):
        buffer[at] = ga_v[send_slot(dest)]

    exchange(fill_ga, ga_s, ga_r, 1)

    factor = 0.1 * math.log(yarn_factor) + 1.0
    sign = jnp.where(lax.broadcasted_iota(jnp.int32, (1, RB), 1) < HD // 2, -factor, factor)
    for b in range(NB):
        mine = jnp.broadcast_to(seg[b : b + 1, :], (RB, RB)).T
        smaller = jnp.zeros((RB, RB), jnp.int32)
        for other in range(b + 1):
            smaller += jnp.where(seg[other : other + 1, :] < mine, 1, 0)
        first = jnp.sum(smaller, axis=1, keepdims=True)
        start[b] = jnp.broadcast_to(first, (RB, RB))

    def tables(b, carry):
        row = b * RB + lax.broadcasted_iota(jnp.int32, (RB, RB), 0)
        angle = (row - start[b]).astype(F32) * freq[0:1, :]
        cosf[b] = jnp.cos(angle) * factor
        sinf[b] = jnp.sin(angle) * sign
        return carry

    lax.fori_loop(0, NB, tables, 0)

    def find(g, carry):
        source = plan[g] - me * NB
        return tuple(jnp.where(source == j, g // NB, carry[j]) for j in range(NB))

    homes = lax.fori_loop(0, RANKS * NB, find, (jnp.int32(0),) * NB)

    def turned(x, cosine, sine):
        return x * cosine + pltpu.roll(x, HD // 2, 1) * sine

    def pair_copy(src, dst, i):
        return pltpu.make_async_remote_copy(
            src_ref=src, dst_ref=dst, send_sem=pair_send.at[i], recv_sem=pair_recv.at[i],
            device_id={"tensor": partner}, device_id_type=MESH,
        )

    all_moved(qkv_s, qkv_r, 0).wait_recv()
    is_key = (core == 0).astype(F32)

    def arrive_kv(b, carry):
        origin = plan[me * NB + b] >> 3
        x = qkv_r[origin][:, COLS:].astype(F32)
        cosine = cosf[b] * is_key + (1.0 - is_key)
        kv2[core, b] = turned(x, cosine, sinf[b] * is_key).astype(BF)
        return carry

    lax.fori_loop(0, NB, arrive_kv, 0)
    share_kv = pair_copy(kv2.at[core], kv2.at[core], 0)
    share_kv.start()

    for b in range(NB):
        block = qkv_r[plan[me * NB + b] >> 3]
        for h in range(2):
            x = block[:, h * HD : (h + 1) * HD].astype(F32)
            part = pl.ds((b % 2) * RB, RB)
            qs[b // 2 * 2 + h, part] = turned(x, cosf[b], sinf[b]).astype(BF)
    share_kv.wait_recv()

    def key_tile(kb):
        return kv2[0, 2 * kb : 2 * kb + 2].reshape(TILE, HD)

    def value_tile(kb):
        return kv2[1, 2 * kb : 2 * kb + 2].reshape(TILE, HD)

    column = lax.broadcasted_iota(jnp.int32, (TILE, TILE), 1)
    row_of = lax.broadcasted_iota(jnp.int32, (TILE, TILE), 0)
    for t in range(TILES):
        first = start[2 * t : 2 * t + 2].reshape(TILE, RB)
        first = jnp.concatenate([first, first], axis=1)

        def forward(h, carry):
            rows = qs[2 * t + h]
            scores = []
            for kb in range(t + 1):
                raw = dot(rows, key_tile(kb), NT)
                allowed = column + kb * TILE >= first
                if kb == t:
                    allowed = allowed & (column <= row_of)
                scores.append(jnp.where(allowed, raw, masked_score))
            peak = functools.reduce(jnp.maximum, scores)
            peak = jnp.max(peak, axis=1, keepdims=True)
            scores = [jnp.exp2((s - peak) * log2_scale) for s in scores]
            total = jnp.sum(functools.reduce(jnp.add, scores), axis=1, keepdims=True)
            share = 1.0 / total
            out = jnp.zeros((TILE, HD), F32)
            for kb in range(t + 1):
                p = scores[kb] * share
                prob[2 * t + h, :, kb * TILE : (kb + 1) * TILE] = p
                out += dot(p.astype(BF), value_tile(kb), NN)
            outs[2 * t : 2 * t + 2, h] = out.astype(BF).reshape(2, RB, HD)
            return carry

        lax.fori_loop(0, 2, forward, 0)

    def fill_out(buffer, at, dest):
        rows = outs[back_slot(dest)]
        for h in range(2):
            buffer[at, :, h * HD : (h + 1) * HD] = rows[h]

    exchange(fill_out, ao_s, ao_r, 2)

    all_moved(ga_s, ga_r, 1).wait_recv()
    for b in range(NB):
        block = ga_r[plan[me * NB + b] >> 3]
        for h in range(2):
            part = pl.ds((b % 2) * RB, RB)
            gas[b // 2 * 2 + h, part] = block[:, h * HD : (h + 1) * HD]

    dkt[...] = jnp.zeros_like(dkt)
    dvt[...] = jnp.zeros_like(dvt)
    for t in range(TILES):
        cosine = cosf[2 * t : 2 * t + 2].reshape(TILE, HD)
        sine = sinf[2 * t : 2 * t + 2].reshape(TILE, HD)

        def backward(h, carry):
            u = 2 * t + h
            upstream = gas[u]
            rows = qs[u]
            out = outs[2 * t : 2 * t + 2, h].reshape(TILE, HD)
            delta = jnp.sum(
                upstream.astype(F32) * out.astype(F32), axis=1, keepdims=True
            )
            dq = jnp.zeros((TILE, HD), F32)
            for kb in range(t + 1):
                cols = slice(kb * TILE, (kb + 1) * TILE)
                p = prob[u, :, cols]
                dp = dot(upstream, value_tile(kb), NT)
                ds = (p * (dp - delta)).astype(BF)
                dq += dot(ds, key_tile(kb), NN)
                dkt[:, cols] += dot(rows, ds, TN)
                dvt[:, cols] += dot(upstream, p.astype(BF), TN)
            dq = turned(dq * inv_scale, cosine, -sine).astype(BF)
            dq_v[2 * t : 2 * t + 2, h] = dq.reshape(2, RB, HD)
            return carry

        lax.fori_loop(0, 2, backward, 0)

    for b in range(NB):
        cols = slice(b * RB, (b + 1) * RB)
        dk = dkt[:, cols].T * inv_scale
        dkv_own[0, b] = turned(dk, cosf[b], -sinf[b]).astype(BF)
        dkv_own[1, b] = dvt[:, cols].T.astype(BF)
    share_dkv = pair_copy(dkv_own.at[1 - core], dkv_in, 1)
    share_dkv.start()

    def fill_dq(buffer, at, dest):
        rows = dq_v[back_slot(dest)]
        for h in range(2):
            buffer[at, :, h * HD : (h + 1) * HD] = rows[h]

    def fill_dkv(buffer, at, dest):
        buffer[at] = dkv_v[back_slot(dest)]

    share_dkv.wait_recv()
    for b in range(NB):
        dkv_v[b] = (dkv_own[core, b].astype(F32) + dkv_in[b].astype(F32)).astype(BF)
    exchange(fill_dkv, dkv_s, dkv_r, 3)
    exchange(fill_dq, dq_s, dq_r, 4)

    all_moved(ao_s, ao_r, 2).wait_recv()
    for j in range(NB):
        aoh[j * RB : (j + 1) * RB] = ao_r[homes[j]]
    chunk = 4 * WROWS
    for c in range(D // chunk):
        rows = g_v[:, :, c * chunk : (c + 1) * chunk].reshape(NB * RB, chunk)
        term = dot(aoh[...], rows, TN).T.astype(BF)
        for e in range(4):
            w_s[4 * c + e] = term[e * WROWS : (e + 1) * WROWS]

    def send_weight(o, carry):
        moved(w_s, w_r, 5, lax.rem(me + o, RANKS)).start()
        return carry

    lax.fori_loop(1, RANKS, send_weight, 0)
    w_r[me] = w_s[me]

    all_moved(dkv_s, dkv_r, 3).wait_recv()
    for j in range(NB):
        zk[core, zed, j] = dkv_r[homes[j]]
    z_copies = []
    for o in range(1, 4):
        copy = pltpu.make_async_remote_copy(
            src_ref=zk.at[core, zed], dst_ref=zk.at[core, zed],
            send_sem=z_send.at[o - 1], recv_sem=z_recv.at[o - 1],
            device_id={"tensor": lax.rem(zed + o, 4) * 2 + core}, device_id_type=MESH,
        )
        copy.start()
        z_copies.append(copy)

    all_moved(dq_s, dq_r, 4).wait_recv()
    for j in range(NB):
        q_v[j] = dq_r[homes[j]]
    gq_out = pltpu.make_async_copy(q_v, gq_hbm, out_sem.at[0])
    gq_out.start()

    for copy in z_copies:
        copy.wait_recv()
    share_z = pair_copy(zk.at[core], zk.at[core], 2)
    share_z.start()
    share_z.wait_recv()
    copies = []
    for k, target in enumerate((gk_hbm, gv_hbm)):
        for z in range(KV):
            copy = pltpu.make_async_copy(
                zk.at[k, z], target.at[:, :, z * HD : (z + 1) * HD], out_sem.at[1 + 4 * k + z]
            )
            copy.start()
            copies.append(copy)

    all_moved(w_s, w_r, 5).wait_recv()
    total = jnp.zeros((WROWS, COLS), F32)
    for r in range(RANKS):
        total += w_r[r].astype(F32)
    gw_v[...] = total * (1.0 / RANKS)
    gw_out = pltpu.make_async_copy(gw_v, gw_hbm, out_sem.at[9])
    gw_out.start()

    for kind, (stage, landing) in enumerate(
        ((qkv_s, qkv_r), (ga_s, ga_r), (ao_s, ao_r), (dkv_s, dkv_r), (dq_s, dq_r), (w_s, w_r))
    ):
        all_moved(stage, landing, kind).wait_send()
    share_kv.wait_send()
    share_dkv.wait_send()
    share_z.wait_send()
    for copy in z_copies:
        copy.wait_send()
    gq_out.wait()
    for copy in copies:
        copy.wait()
    gw_out.wait()


def local(query, key, value, grad_out, out_weight, plan, segments):
    blocked = (NB, RB)
    half = yarn_frequencies(HD)
    freq = jnp.broadcast_to(jnp.concatenate([half, half])[None, :], (8, HD))
    hbm = pl.BlockSpec(memory_space=pl.ANY)
    vmem = pl.BlockSpec(memory_space=pltpu.VMEM)
    V = pltpu.VMEM
    dma = pltpu.SemaphoreType.DMA
    rows = NB * RB
    gq, gk, gv, gw = pl.pallas_call(
        kernel,
        out_shape=(
            jax.ShapeDtypeStruct(blocked + (COLS,), BF),
            jax.ShapeDtypeStruct(blocked + (KV * HD,), BF),
            jax.ShapeDtypeStruct(blocked + (KV * HD,), BF),
            jax.ShapeDtypeStruct((WROWS, COLS), F32),
        ),
        in_specs=[pl.BlockSpec(memory_space=pltpu.SMEM), vmem, vmem] + [hbm] * 5,
        out_specs=(hbm,) * 4,
        scratch_shapes=[
            V(blocked + (COLS,), BF),
            V(blocked + (HD,), BF),
            V(blocked + (D,), BF),
            V((D, COLS), BF),
            V((RANKS, RB, COLS + HD), BF),
            V((RANKS, RB, COLS + HD), BF),
            V(blocked + (COLS,), BF),
            V((RANKS, RB, COLS), BF),
            V((RANKS, RB, COLS), BF),
            V((2,) + blocked + (HD,), BF),
            V((2 * TILES, TILE, HD), BF),
            V((2 * TILES, TILE, HD), BF),
            V((NB, 2, RB, HD), BF),
            V((2 * TILES, TILE, rows), F32),
            V((RANKS, RB, COLS), BF),
            V((RANKS, RB, COLS), BF),
            V((NB, 2, RB, HD), BF),
            V((RANKS, RB, COLS), BF),
            V((RANKS, RB, COLS), BF),
            V((HD, rows), F32),
            V((HD, rows), F32),
            V((2,) + blocked + (HD,), BF),
            V(blocked + (HD,), BF),
            V(blocked + (HD,), BF),
            V((RANKS, RB, HD), BF),
            V((RANKS, RB, HD), BF),
            V((RANKS, WROWS, COLS), BF),
            V((RANKS, WROWS, COLS), BF),
            V((2, KV) + blocked + (HD,), BF),
            V((rows, COLS), BF),
            V((WROWS, COLS), F32),
            V(blocked + (HD,), F32),
            V(blocked + (HD,), F32),
            V(blocked + (RB,), jnp.int32),
            dma((3,)),
            dma((TILES,)),
            dma((6,)),
            dma((6,)),
            dma((3,)),
            dma((3,)),
            dma((3,)),
            dma((3,)),
            dma((10,)),
        ],
        compiler_params=pltpu.CompilerParams(
            collective_id=0, has_side_effects=True, vmem_limit_bytes=60 * 2**20
        ),
        cost_estimate=pl.CostEstimate(
            flops=7 * 10**9, bytes_accessed=14 * 2**20, transcendentals=2 * 10**6
        ),
    )(
        plan,
        segments.reshape(NB, RB),
        freq,
        query.reshape(blocked + (COLS,)),
        key.reshape(blocked + (KV * HD,)),
        value.reshape(blocked + (KV * HD,)),
        grad_out.reshape(blocked + (D,)),
        out_weight,
    )
    return (
        gq.reshape(rows, COLS),
        gk.reshape(rows, KV * HD),
        gv.reshape(rows, KV * HD),
        gw,
    )


def solution(mesh):
    in_specs = (
        P("dp", "tensor"),
        P("dp", None),
        P("dp", None),
        P("dp", None),
        P(None, "tensor"),
        P(),
        P("dp"),
    )
    out_specs = (P("dp", "tensor"), P("dp", None), P("dp", None), P("dp", "tensor"))
    return jax.shard_map(local, mesh=mesh, in_specs=in_specs, out_specs=out_specs, check_vma=False)
```

```python
import functools
import math

import jax
import jax.numpy as jnp
import numpy as np
from jax import lax
from jax.experimental import pallas as pl
from jax.experimental.pallas import tpu as pltpu
from jax.sharding import PartitionSpec as P

D = 3584
KV = 4
HD = 128
HEADS = 16
RB = 128
NB = 8
RANKS = 16
LANES = 8
COLS = 256
TILE = 256
TILES = NB * RB // TILE
WROWS = D // RANKS
SIDE = 4
ORDER = (
    (1, 0), (0, 1), (3, 0), (0, 3), (2, 0), (0, 2), (1, 1), (3, 3),
    (1, 3), (3, 1), (2, 2), (1, 2), (2, 1), (3, 2), (2, 3),
)
DX = sum(dx << (2 * i) for i, (dx, dy) in enumerate(ORDER))
DY = sum(dy << (2 * i) for i, (dx, dy) in enumerate(ORDER))

rope_base = 1000000.0
yarn_factor = 4.0
yarn_context = 32768.0
beta_fast = 32.0
beta_slow = 1.0
masked_score = -1e30
MESH = pl.DeviceIdType.MESH
BF = jnp.bfloat16
F32 = jnp.float32


def yarn_frequencies(head_size):
    half_size = head_size // 2

    def correction(rotations):
        return (
            head_size
            * math.log(yarn_context / (rotations * 2.0 * math.pi))
            / (2.0 * math.log(rope_base))
        )

    lower_bound = max(math.floor(correction(beta_fast)), 0)
    upper_bound = min(math.ceil(correction(beta_slow)), head_size - 1)
    ramp_span = max(upper_bound - lower_bound, 0.001)
    row_index = np.arange(half_size).astype(np.float64)
    extrap_freq = rope_base ** (-2.0 * row_index / head_size)
    interp_freq = extrap_freq / yarn_factor
    ramp_weight = np.clip((row_index - lower_bound) / ramp_span, 0.0, 1.0)
    return interp_freq * ramp_weight + extrap_freq * (1.0 - ramp_weight)


def dot(a, b, dims):
    return lax.dot_general(a, b, (dims, ((), ())), preferred_element_type=F32)


NN = ((1,), (0,))
NT = ((1,), (1,))
TN = ((0,), (0,))


def kernel(
    plan, seg, freq, q_hbm, k_hbm, v_hbm, g_hbm, w_hbm,
    gq_hbm, gk_hbm, gv_hbm, gw_hbm,
    q_v, kv_v, g_v, w_v, qkv_s, qkv_r, ga_v, ga_s, ga_r, kv2, qs, gas, outs, prob,
    ao_s, ao_r, dq_v, dq_s, dq_r, dkt, dvt, dkv_own, dkv_in, dkv_v, dkv_s, dkv_r,
    w_s, w_r, w2_s, w2_r, zk, aoh, gw_v, cosf, sinf, start,
    in_sem, g_sem, send_sem, recv_sem, pair_send, pair_recv, z_send, z_recv, w_send, w_recv, out_sem,
):
    me = lax.axis_index("dp")
    lane = lax.axis_index("tensor")
    core = lax.rem(lane, 2)
    zed = lane // 2
    partner = lane + 1 - 2 * core
    my_x = me // SIDE
    my_y = lax.rem(me, SIDE)
    inv_scale = 1.0 / math.sqrt(HD)
    log2_scale = inv_scale * math.log2(math.e)

    barrier = pltpu.get_barrier_semaphore()

    def greet(o, carry):
        pl.semaphore_signal(
            barrier, inc=1, device_id={"dp": lax.rem(me + o, RANKS)}, device_id_type=MESH
        )
        return carry

    lax.fori_loop(1, RANKS, greet, 0)
    pl.semaphore_signal(barrier, inc=1, device_id={"tensor": partner}, device_id_type=MESH)
    for o in range(1, 4):
        peer = lax.rem(zed + o, 4) * 2 + core
        pl.semaphore_signal(barrier, inc=1, device_id={"tensor": peer}, device_id_type=MESH)

    q_in = pltpu.make_async_copy(q_hbm, q_v, in_sem.at[0])
    q_in.start()
    head_cols = pl.ds(pl.multiple_of(zed * HD, HD), HD)
    k_in = pltpu.make_async_copy(k_hbm.at[:, :, head_cols], kv_v, in_sem.at[1])
    v_in = pltpu.make_async_copy(v_hbm.at[:, :, head_cols], kv_v, in_sem.at[1])
    pl.when(core == 0)(k_in.start)
    pl.when(core == 1)(v_in.start)
    w_in = pltpu.make_async_copy(w_hbm, w_v, in_sem.at[2])
    w_in.start()
    g_in = [
        pltpu.make_async_copy(
            g_hbm.at[pl.ds(2 * t, 2)], g_v.at[pl.ds(2 * t, 2)], g_sem.at[t]
        )
        for t in range(TILES)
    ]
    for copy in g_in:
        copy.start()

    def send_slot(dest):
        slot = jnp.int32(0)
        for b in range(NB):
            source = plan[dest * NB + b]
            slot = jnp.where((source >> 3) == me, source & 7, slot)
        return slot

    def back_slot(dest):
        slot = jnp.int32(0)
        for b in range(NB):
            slot = jnp.where((plan[me * NB + b] >> 3) == dest, b, slot)
        return slot

    def moved(stage, landing, kind, dest):
        return pltpu.make_async_remote_copy(
            src_ref=stage.at[dest],
            dst_ref=landing.at[me],
            send_sem=send_sem.at[kind],
            recv_sem=recv_sem.at[kind],
            device_id={"dp": dest},
            device_id_type=MESH,
        )

    def all_moved(stage, landing, kind):
        rest = pl.ds(0, RANKS - 1)
        return pltpu.make_async_remote_copy(
            src_ref=stage.at[rest],
            dst_ref=landing.at[rest],
            send_sem=send_sem.at[kind],
            recv_sem=recv_sem.at[kind],
            device_id={"dp": lax.rem(me + 1, RANKS)},
            device_id_type=MESH,
        )

    def exchange(fill, stage, landing, kind):
        def one(o, carry):
            dxs, dys = carry
            x = lax.rem(my_x + lax.rem(dxs, SIDE), SIDE)
            y = lax.rem(my_y + lax.rem(dys, SIDE), SIDE)
            dest = x * SIDE + y
            fill(stage, dest, dest)
            moved(stage, landing, kind, dest).start()
            return dxs // SIDE, dys // SIDE

        lax.fori_loop(1, RANKS, one, (jnp.int32(DX), jnp.int32(DY)))
        fill(landing, me, me)

    q_in.wait()
    pl.when(core == 0)(k_in.wait)
    pl.when(core == 1)(v_in.wait)
    pl.semaphore_wait(barrier, RANKS - 1 + 4)

    def fill_qkv(buffer, at, dest):
        slot = send_slot(dest)
        buffer[at, :, :COLS] = q_v[slot]
        buffer[at, :, COLS:] = kv_v[slot]

    exchange(fill_qkv, qkv_s, qkv_r, 0)

    w_in.wait()
    for t in range(TILES):
        g_in[t].wait()
    def project(t, carry):
        rows = pl.ds(2 * t, 2)
        product = dot(g_v[rows].reshape(TILE, D), w_v[...], NN)
        ga_v[rows] = product.astype(BF).reshape(2, RB, COLS)
        return carry

    lax.fori_loop(0, TILES, project, 0)

    def fill_ga(buffer, at, dest):
        buffer[at] = ga_v[send_slot(dest)]

    exchange(fill_ga, ga_s, ga_r, 1)

    factor = 0.1 * math.log(yarn_factor) + 1.0
    sign = jnp.where(lax.broadcasted_iota(jnp.int32, (1, RB), 1) < HD // 2, -factor, factor)
    for b in range(NB):
        mine = jnp.broadcast_to(seg[b : b + 1, :], (RB, RB)).T
        smaller = jnp.zeros((RB, RB), jnp.int32)
        for other in range(b + 1):
            smaller += jnp.where(seg[other : other + 1, :] < mine, 1, 0)
        first = jnp.sum(smaller, axis=1, keepdims=True)
        start[b] = jnp.broadcast_to(first, (RB, RB))

    def tables(b, carry):
        row = b * RB + lax.broadcasted_iota(jnp.int32, (RB, RB), 0)
        angle = (row - start[b]).astype(F32) * freq[0:1, :]
        cosf[b] = jnp.cos(angle) * factor
        sinf[b] = jnp.sin(angle) * sign
        return carry

    lax.fori_loop(0, NB, tables, 0)

    def find(g, carry):
        source = plan[g] - me * NB
        return tuple(jnp.where(source == j, g // NB, carry[j]) for j in range(NB))

    homes = lax.fori_loop(0, RANKS * NB, find, (jnp.int32(0),) * NB)

    def turned(x, cosine, sine):
        return x * cosine + pltpu.roll(x, HD // 2, 1) * sine

    def pair_copy(src, dst, i):
        return pltpu.make_async_remote_copy(
            src_ref=src, dst_ref=dst, send_sem=pair_send.at[i], recv_sem=pair_recv.at[i],
            device_id={"tensor": partner}, device_id_type=MESH,
        )

    all_moved(qkv_s, qkv_r, 0).wait_recv()
    is_key = (core == 0).astype(F32)

    def arrive_kv(b, carry):
        origin = plan[me * NB + b] >> 3
        x = qkv_r[origin][:, COLS:].astype(F32)
        cosine = cosf[b] * is_key + (1.0 - is_key)
        kv2[core, b] = turned(x, cosine, sinf[b] * is_key).astype(BF)
        return carry

    lax.fori_loop(0, NB, arrive_kv, 0)
    share_kv = pair_copy(kv2.at[core], kv2.at[core], 0)
    share_kv.start()

    for b in range(NB):
        block = qkv_r[plan[me * NB + b] >> 3]
        for h in range(2):
            x = block[:, h * HD : (h + 1) * HD].astype(F32)
            part = pl.ds((b % 2) * RB, RB)
            qs[b // 2 * 2 + h, part] = turned(x, cosf[b], sinf[b]).astype(BF)
    share_kv.wait_recv()

    def key_tile(kb):
        return kv2[0, 2 * kb : 2 * kb + 2].reshape(TILE, HD)

    def value_tile(kb):
        return kv2[1, 2 * kb : 2 * kb + 2].reshape(TILE, HD)

    column = lax.broadcasted_iota(jnp.int32, (TILE, TILE), 1)
    row_of = lax.broadcasted_iota(jnp.int32, (TILE, TILE), 0)
    for t in range(TILES):
        first = start[2 * t : 2 * t + 2].reshape(TILE, RB)
        first = jnp.concatenate([first, first], axis=1)

        def forward(h, carry):
            rows = qs[2 * t + h]
            scores = []
            for kb in range(t + 1):
                raw = dot(rows, key_tile(kb), NT)
                allowed = column + kb * TILE >= first
                if kb == t:
                    allowed = allowed & (column <= row_of)
                scores.append(jnp.where(allowed, raw, masked_score))
            peak = functools.reduce(jnp.maximum, scores)
            peak = jnp.max(peak, axis=1, keepdims=True)
            scores = [jnp.exp2((s - peak) * log2_scale) for s in scores]
            total = jnp.sum(functools.reduce(jnp.add, scores), axis=1, keepdims=True)
            share = 1.0 / total
            out = jnp.zeros((TILE, HD), F32)
            for kb in range(t + 1):
                p = scores[kb] * share
                prob[2 * t + h, :, kb * TILE : (kb + 1) * TILE] = p
                out += dot(p.astype(BF), value_tile(kb), NN)
            outs[2 * t : 2 * t + 2, h] = out.astype(BF).reshape(2, RB, HD)
            return carry

        lax.fori_loop(0, 2, forward, 0)

    def fill_out(buffer, at, dest):
        rows = outs[back_slot(dest)]
        for h in range(2):
            buffer[at, :, h * HD : (h + 1) * HD] = rows[h]

    exchange(fill_out, ao_s, ao_r, 2)

    all_moved(ga_s, ga_r, 1).wait_recv()
    for b in range(NB):
        block = ga_r[plan[me * NB + b] >> 3]
        for h in range(2):
            part = pl.ds((b % 2) * RB, RB)
            gas[b // 2 * 2 + h, part] = block[:, h * HD : (h + 1) * HD]

    dkt[...] = jnp.zeros_like(dkt)
    dvt[...] = jnp.zeros_like(dvt)
    for t in range(TILES):
        cosine = cosf[2 * t : 2 * t + 2].reshape(TILE, HD)
        sine = sinf[2 * t : 2 * t + 2].reshape(TILE, HD)

        def backward(h, carry):
            u = 2 * t + h
            upstream = gas[u]
            rows = qs[u]
            out = outs[2 * t : 2 * t + 2, h].reshape(TILE, HD)
            delta = jnp.sum(
                upstream.astype(F32) * out.astype(F32), axis=1, keepdims=True
            )
            dq = jnp.zeros((TILE, HD), F32)
            for kb in range(t + 1):
                cols = slice(kb * TILE, (kb + 1) * TILE)
                p = prob[u, :, cols]
                dp = dot(upstream, value_tile(kb), NT)
                ds = (p * (dp - delta)).astype(BF)
                dq += dot(ds, key_tile(kb), NN)
                dkt[:, cols] += dot(rows, ds, TN)
                dvt[:, cols] += dot(upstream, p.astype(BF), TN)
            dq = turned(dq * inv_scale, cosine, -sine).astype(BF)
            dq_v[2 * t : 2 * t + 2, h] = dq.reshape(2, RB, HD)
            return carry

        lax.fori_loop(0, 2, backward, 0)

    for b in range(NB):
        cols = slice(b * RB, (b + 1) * RB)
        dk = dkt[:, cols].T * inv_scale
        dkv_own[0, b] = turned(dk, cosf[b], -sinf[b]).astype(BF)
        dkv_own[1, b] = dvt[:, cols].T.astype(BF)
    share_dkv = pair_copy(dkv_own.at[1 - core], dkv_in, 1)
    share_dkv.start()

    def fill_dq(buffer, at, dest):
        rows = dq_v[back_slot(dest)]
        for h in range(2):
            buffer[at, :, h * HD : (h + 1) * HD] = rows[h]

    def fill_dkv(buffer, at, dest):
        buffer[at] = dkv_v[back_slot(dest)]

    share_dkv.wait_recv()
    for b in range(NB):
        dkv_v[b] = (dkv_own[core, b].astype(F32) + dkv_in[b].astype(F32)).astype(BF)
    exchange(fill_dkv, dkv_s, dkv_r, 3)

    all_moved(ao_s, ao_r, 2).wait_recv()
    for j in range(NB):
        aoh[j * RB : (j + 1) * RB] = ao_r[homes[j]]
    chunk = SIDE * WROWS
    for c in range(SIDE):
        rows = g_v[:, :, c * chunk : (c + 1) * chunk].reshape(NB * RB, chunk)
        term = dot(aoh[...], rows, TN).T.astype(BF)
        for e in range(SIDE):
            part = term[e * WROWS : (e + 1) * WROWS]
            w_s[0, c, e] = part[:, :HD]
            w_s[1, e, c] = part[:, HD:]

    mine = (my_x, my_y)

    def along(half, step, o):
        axis = half if step == 0 else 1 - half
        to = lax.rem(mine[axis] + o, SIDE)
        dest = to * SIDE + my_y if axis == 0 else my_x * SIDE + to
        stage, landing = ((w_s, w_r), (w2_s, w2_r))[step]
        return pltpu.make_async_remote_copy(
            src_ref=stage.at[half, to], dst_ref=landing.at[half, mine[axis]],
            send_sem=w_send.at[step, half, o - 1], recv_sem=w_recv.at[step, half, o - 1],
            device_id={"dp": dest}, device_id_type=MESH,
        )

    w_copies = [[along(half, step, o) for o in (1, 3, 2) for half in range(2)] for step in range(2)]
    for copy in w_copies[0]:
        copy.start()
    for half in range(2):
        w_r[half, mine[half]] = w_s[half, mine[half]]
    exchange(fill_dq, dq_s, dq_r, 4)

    all_moved(dkv_s, dkv_r, 3).wait_recv()
    for j in range(NB):
        zk[core, zed, j] = dkv_r[homes[j]]
    z_copies = []
    for o in range(1, 4):
        copy = pltpu.make_async_remote_copy(
            src_ref=zk.at[core, zed], dst_ref=zk.at[core, zed],
            send_sem=z_send.at[o - 1], recv_sem=z_recv.at[o - 1],
            device_id={"tensor": lax.rem(zed + o, 4) * 2 + core}, device_id_type=MESH,
        )
        copy.start()
        z_copies.append(copy)

    for copy in w_copies[0]:
        copy.wait_recv()
    for half in range(2):
        for e in range(SIDE):
            total = jnp.zeros((WROWS, HD), F32)
            for r in range(SIDE):
                total += w_r[half, r, e].astype(F32)
            w2_s[half, e] = total.astype(BF)
    for copy in w_copies[1]:
        copy.start()
    for half in range(2):
        w2_r[half, mine[1 - half]] = w2_s[half, mine[1 - half]]

    all_moved(dq_s, dq_r, 4).wait_recv()
    for j in range(NB):
        q_v[j] = dq_r[homes[j]]
    gq_out = pltpu.make_async_copy(q_v, gq_hbm, out_sem.at[0])
    gq_out.start()

    for copy in z_copies:
        copy.wait_recv()
    share_z = pair_copy(zk.at[core], zk.at[core], 2)
    share_z.start()
    share_z.wait_recv()
    copies = []
    for k, target in enumerate((gk_hbm, gv_hbm)):
        for z in range(KV):
            copy = pltpu.make_async_copy(
                zk.at[k, z], target.at[:, :, z * HD : (z + 1) * HD], out_sem.at[1 + 4 * k + z]
            )
            copy.start()
            copies.append(copy)

    for copy in w_copies[1]:
        copy.wait_recv()
    for half in range(2):
        total = jnp.zeros((WROWS, HD), F32)
        for r in range(SIDE):
            total += w2_r[half, r].astype(F32)
        gw_v[:, half * HD : (half + 1) * HD] = total * (1.0 / RANKS)
    gw_out = pltpu.make_async_copy(gw_v, gw_hbm, out_sem.at[9])
    gw_out.start()

    for kind, (stage, landing) in enumerate(
        ((qkv_s, qkv_r), (ga_s, ga_r), (ao_s, ao_r), (dkv_s, dkv_r), (dq_s, dq_r))
    ):
        all_moved(stage, landing, kind).wait_send()
    for copy in w_copies[0] + w_copies[1]:
        copy.wait_send()
    share_kv.wait_send()
    share_dkv.wait_send()
    share_z.wait_send()
    for copy in z_copies:
        copy.wait_send()
    gq_out.wait()
    for copy in copies:
        copy.wait()
    gw_out.wait()


def hand_on(*refs):
    source, target, held, sems = refs[:4], refs[4:8], refs[8:12], refs[12]
    parts = []
    for k in range(4):
        half = source[k].shape[0] // 2
        for h in range(2):
            part = pl.ds(h * half, half)
            sem = sems.at[2 * k + h]
            parts.append(
                (
                    pltpu.make_async_copy(source[k].at[part], held[k].at[part], sem),
                    pltpu.make_async_copy(held[k].at[part], target[k].at[part], sem),
                )
            )
    for load, store in parts:
        load.start()
    for load, store in parts:
        load.wait()
        store.start()
    for load, store in parts:
        store.wait()


def local(query, key, value, grad_out, out_weight, plan, segments):
    blocked = (NB, RB)
    half = yarn_frequencies(HD)
    freq = np.tile(np.concatenate([half, half]), (8, 1)).astype(np.float32)
    hbm = pl.BlockSpec(memory_space=pl.ANY)
    vmem = pl.BlockSpec(memory_space=pltpu.VMEM)
    V = pltpu.VMEM
    dma = pltpu.SemaphoreType.DMA
    rows = NB * RB
    gq, gk, gv, gw = pl.pallas_call(
        kernel,
        out_shape=(
            jax.ShapeDtypeStruct(blocked + (COLS,), BF),
            jax.ShapeDtypeStruct(blocked + (KV * HD,), BF),
            jax.ShapeDtypeStruct(blocked + (KV * HD,), BF),
            jax.ShapeDtypeStruct((WROWS, COLS), F32),
        ),
        in_specs=[pl.BlockSpec(memory_space=pltpu.SMEM), vmem, vmem] + [hbm] * 5,
        out_specs=(hbm,) * 4,
        scratch_shapes=[
            V(blocked + (COLS,), BF),
            V(blocked + (HD,), BF),
            V(blocked + (D,), BF),
            V((D, COLS), BF),
            V((RANKS, RB, COLS + HD), BF),
            V((RANKS, RB, COLS + HD), BF),
            V(blocked + (COLS,), BF),
            V((RANKS, RB, COLS), BF),
            V((RANKS, RB, COLS), BF),
            V((2,) + blocked + (HD,), BF),
            V((2 * TILES, TILE, HD), BF),
            V((2 * TILES, TILE, HD), BF),
            V((NB, 2, RB, HD), BF),
            V((2 * TILES, TILE, rows), F32),
            V((RANKS, RB, COLS), BF),
            V((RANKS, RB, COLS), BF),
            V((NB, 2, RB, HD), BF),
            V((RANKS, RB, COLS), BF),
            V((RANKS, RB, COLS), BF),
            V((HD, rows), F32),
            V((HD, rows), F32),
            V((2,) + blocked + (HD,), BF),
            V(blocked + (HD,), BF),
            V(blocked + (HD,), BF),
            V((RANKS, RB, HD), BF),
            V((RANKS, RB, HD), BF),
            V((2, SIDE, SIDE, WROWS, HD), BF),
            V((2, SIDE, SIDE, WROWS, HD), BF),
            V((2, SIDE, WROWS, HD), BF),
            V((2, SIDE, WROWS, HD), BF),
            V((2, KV) + blocked + (HD,), BF),
            V((rows, COLS), BF),
            V((WROWS, COLS), F32),
            V(blocked + (HD,), F32),
            V(blocked + (HD,), F32),
            V(blocked + (RB,), jnp.int32),
            dma((3,)),
            dma((TILES,)),
            dma((5,)),
            dma((5,)),
            dma((3,)),
            dma((3,)),
            dma((3,)),
            dma((3,)),
            dma((2, 2, 3)),
            dma((2, 2, 3)),
            dma((10,)),
        ],
        compiler_params=pltpu.CompilerParams(
            collective_id=0, has_side_effects=True, vmem_limit_bytes=60 * 2**20
        ),
        cost_estimate=pl.CostEstimate(
            flops=7 * 10**9, bytes_accessed=14 * 2**20, transcendentals=2 * 10**6
        ),
    )(
        plan,
        segments.reshape(NB, RB),
        freq,
        query.reshape(blocked + (COLS,)),
        key.reshape(blocked + (KV * HD,)),
        value.reshape(blocked + (KV * HD,)),
        grad_out.reshape(blocked + (D,)),
        out_weight,
    )
    gq, gk, gv, gw = pl.pallas_call(
        hand_on,
        out_shape=tuple(jax.ShapeDtypeStruct(x.shape, x.dtype) for x in (gq, gk, gv, gw)),
        in_specs=[hbm] * 4,
        out_specs=(hbm,) * 4,
        scratch_shapes=[V(x.shape, x.dtype) for x in (gq, gk, gv, gw)] + [dma((8,))],
    )(gq, gk, gv, gw)
    return (
        gq.reshape(rows, COLS),
        gk.reshape(rows, KV * HD),
        gv.reshape(rows, KV * HD),
        gw,
    )


def solution(mesh):
    in_specs = (
        P("dp", "tensor"),
        P("dp", None),
        P("dp", None),
        P("dp", None),
        P(None, "tensor"),
        P(),
        P("dp"),
    )
    out_specs = (P("dp", "tensor"), P("dp", None), P("dp", None), P("dp", "tensor"))
    return jax.shard_map(local, mesh=mesh, in_specs=in_specs, out_specs=out_specs, check_vma=False)
```

```python
import functools
import math

import jax
import jax.numpy as jnp
import numpy as np
from jax import lax
from jax.experimental import pallas as pl
from jax.experimental.pallas import tpu as pltpu
from jax.sharding import PartitionSpec as P

D = 3584
KV = 4
HD = 128
HEADS = 16
RB = 128
NB = 8
RANKS = 16
LANES = 8
COLS = 256
TILE = 256
TILES = NB * RB // TILE
WROWS = D // RANKS
SIDE = 4
ORDER = (
    (1, 0), (0, 1), (3, 3), (2, 0), (0, 3), (1, 1), (3, 0), (0, 2),
    (1, 3), (3, 1), (2, 2), (1, 2), (2, 3), (3, 2), (2, 1),
)
DX = sum(dx << (2 * i) for i, (dx, dy) in enumerate(ORDER))
DY = sum(dy << (2 * i) for i, (dx, dy) in enumerate(ORDER))

rope_base = 1000000.0
yarn_factor = 4.0
yarn_context = 32768.0
beta_fast = 32.0
beta_slow = 1.0
masked_score = -1e30
MESH = pl.DeviceIdType.MESH
BF = jnp.bfloat16
F32 = jnp.float32


def yarn_frequencies(head_size):
    half_size = head_size // 2

    def correction(rotations):
        return (
            head_size
            * math.log(yarn_context / (rotations * 2.0 * math.pi))
            / (2.0 * math.log(rope_base))
        )

    lower_bound = max(math.floor(correction(beta_fast)), 0)
    upper_bound = min(math.ceil(correction(beta_slow)), head_size - 1)
    ramp_span = max(upper_bound - lower_bound, 0.001)
    row_index = np.arange(half_size).astype(np.float64)
    extrap_freq = rope_base ** (-2.0 * row_index / head_size)
    interp_freq = extrap_freq / yarn_factor
    ramp_weight = np.clip((row_index - lower_bound) / ramp_span, 0.0, 1.0)
    return interp_freq * ramp_weight + extrap_freq * (1.0 - ramp_weight)


def dot(a, b, dims):
    return lax.dot_general(a, b, (dims, ((), ())), preferred_element_type=F32)


NN = ((1,), (0,))
NT = ((1,), (1,))
TN = ((0,), (0,))


def kernel(
    plan, seg, freq, q_hbm, k_hbm, v_hbm, g_hbm, w_hbm,
    gq_hbm, gk_hbm, gv_hbm, gw_hbm,
    q_v, kv_v, g_v, w_v, q_s, q_r, kv_s, kv_r, ga_v, ga_s, ga_r, kv2, qs, gas, outs, prob,
    ao_s, ao_r, dq_v, dq_s, dq_r, dkt, dvt, dkv_own, dkv_in, dkv_v, dkv_s, dkv_r,
    w_s, w_r, w2_s, w2_r, zk, aoh, gw_v, cosf, sinf, start,
    in_sem, g_sem, send_sem, recv_sem, pair_send, pair_recv, z_send, z_recv, w_send, w_recv, out_sem,
):
    me = lax.axis_index("dp")
    lane = lax.axis_index("tensor")
    core = lax.rem(lane, 2)
    zed = lane // 2
    partner = lane + 1 - 2 * core
    my_x = me // SIDE
    my_y = lax.rem(me, SIDE)
    inv_scale = 1.0 / math.sqrt(HD)
    log2_scale = inv_scale * math.log2(math.e)

    barrier = pltpu.get_barrier_semaphore()

    def greet(o, carry):
        pl.semaphore_signal(
            barrier, inc=1, device_id={"dp": lax.rem(me + o, RANKS)}, device_id_type=MESH
        )
        return carry

    lax.fori_loop(1, RANKS, greet, 0)
    pl.semaphore_signal(barrier, inc=1, device_id={"tensor": partner}, device_id_type=MESH)
    for o in range(1, 4):
        peer = lax.rem(zed + o, 4) * 2 + core
        pl.semaphore_signal(barrier, inc=1, device_id={"tensor": peer}, device_id_type=MESH)

    q_in = pltpu.make_async_copy(q_hbm, q_v, in_sem.at[0])
    q_in.start()
    head_cols = pl.ds(pl.multiple_of(zed * HD, HD), HD)
    k_in = pltpu.make_async_copy(k_hbm.at[:, :, head_cols], kv_v, in_sem.at[1])
    v_in = pltpu.make_async_copy(v_hbm.at[:, :, head_cols], kv_v, in_sem.at[1])
    pl.when(core == 0)(k_in.start)
    pl.when(core == 1)(v_in.start)
    w_in = pltpu.make_async_copy(w_hbm, w_v, in_sem.at[2])
    w_in.start()
    g_in = [
        pltpu.make_async_copy(
            g_hbm.at[pl.ds(2 * t, 2)], g_v.at[pl.ds(2 * t, 2)], g_sem.at[t]
        )
        for t in range(TILES)
    ]
    for copy in g_in:
        copy.start()

    def send_slot(dest):
        slot = jnp.int32(0)
        for b in range(NB):
            source = plan[dest * NB + b]
            slot = jnp.where((source >> 3) == me, source & 7, slot)
        return slot

    def back_slot(dest):
        slot = jnp.int32(0)
        for b in range(NB):
            slot = jnp.where((plan[me * NB + b] >> 3) == dest, b, slot)
        return slot

    def moved(stage, landing, kind, dest, h):
        return pltpu.make_async_remote_copy(
            src_ref=stage.at[dest, pl.ds(64 * h, 64)],
            dst_ref=landing.at[me, pl.ds(64 * h, 64)],
            send_sem=send_sem.at[kind],
            recv_sem=recv_sem.at[kind],
            device_id={"dp": dest},
            device_id_type=MESH,
        )

    def all_moved(stage, landing, kind):
        rest = pl.ds(0, RANKS - 1)
        return pltpu.make_async_remote_copy(
            src_ref=stage.at[rest],
            dst_ref=landing.at[rest],
            send_sem=send_sem.at[kind],
            recv_sem=recv_sem.at[kind],
            device_id={"dp": lax.rem(me + 1, RANKS)},
            device_id_type=MESH,
        )

    def round_of(stage, landing, kind, half, fill):
        def one(o, carry):
            dxs, dys = carry
            x = lax.rem(my_x + lax.rem(dxs, SIDE), SIDE)
            y = lax.rem(my_y + lax.rem(dys, SIDE), SIDE)
            dest = x * SIDE + y
            if half == 0:
                fill(stage, dest, dest)
            moved(stage, landing, kind, dest, half).start()
            return dxs // SIDE, dys // SIDE

        lax.fori_loop(1, RANKS, one, (DX + core * (DY - DX), DY + core * (DX - DY)))
        if half == 0:
            fill(landing, me, me)

    def exchange(fill, stage, landing, kind):
        for half in range(2):
            round_of(stage, landing, kind, half, fill)

    pl.when(core == 0)(k_in.wait)
    pl.when(core == 1)(v_in.wait)
    pl.semaphore_wait(barrier, RANKS - 1 + 4)

    def fill_kv(buffer, at, dest):
        buffer[at] = kv_v[send_slot(dest)]

    exchange(fill_kv, kv_s, kv_r, 5)

    q_in.wait()

    def fill_q(buffer, at, dest):
        buffer[at] = q_v[send_slot(dest)]

    exchange(fill_q, q_s, q_r, 0)

    w_in.wait()
    for t in range(TILES):
        g_in[t].wait()
    def project(t, carry):
        rows = pl.ds(2 * t, 2)
        product = dot(g_v[rows].reshape(TILE, D), w_v[...], NN)
        ga_v[rows] = product.astype(BF).reshape(2, RB, COLS)
        return carry

    lax.fori_loop(0, TILES, project, 0)

    def fill_ga(buffer, at, dest):
        buffer[at] = ga_v[send_slot(dest)]

    exchange(fill_ga, ga_s, ga_r, 1)

    factor = 0.1 * math.log(yarn_factor) + 1.0
    sign = jnp.where(lax.broadcasted_iota(jnp.int32, (1, RB), 1) < HD // 2, -factor, factor)
    for b in range(NB):
        mine = jnp.broadcast_to(seg[b : b + 1, :], (RB, RB)).T
        smaller = jnp.zeros((RB, RB), jnp.int32)
        for other in range(b + 1):
            smaller += jnp.where(seg[other : other + 1, :] < mine, 1, 0)
        first = jnp.sum(smaller, axis=1, keepdims=True)
        start[b] = jnp.broadcast_to(first, (RB, RB))

    def tables(b, carry):
        row = b * RB + lax.broadcasted_iota(jnp.int32, (RB, RB), 0)
        angle = (row - start[b]).astype(F32) * freq[0:1, :]
        cosf[b] = jnp.cos(angle) * factor
        sinf[b] = jnp.sin(angle) * sign
        return carry

    lax.fori_loop(0, NB, tables, 0)

    def find(g, carry):
        source = plan[g] - me * NB
        return tuple(jnp.where(source == j, g // NB, carry[j]) for j in range(NB))

    homes = lax.fori_loop(0, RANKS * NB, find, (jnp.int32(0),) * NB)

    def turned(x, cosine, sine):
        return x * cosine + pltpu.roll(x, HD // 2, 1) * sine

    def pair_copy(src, dst, i):
        return pltpu.make_async_remote_copy(
            src_ref=src, dst_ref=dst, send_sem=pair_send.at[i], recv_sem=pair_recv.at[i],
            device_id={"tensor": partner}, device_id_type=MESH,
        )

    all_moved(kv_s, kv_r, 5).wait_recv()
    is_key = (core == 0).astype(F32)

    def arrive_kv(b, carry):
        origin = plan[me * NB + b] >> 3
        x = kv_r[origin].astype(F32)
        cosine = cosf[b] * is_key + (1.0 - is_key)
        kv2[core, b] = turned(x, cosine, sinf[b] * is_key).astype(BF)
        return carry

    lax.fori_loop(0, NB, arrive_kv, 0)
    share_kv = pair_copy(kv2.at[core], kv2.at[core], 0)
    share_kv.start()

    all_moved(q_s, q_r, 0).wait_recv()
    for b in range(NB):
        block = q_r[plan[me * NB + b] >> 3]
        for h in range(2):
            x = block[:, h * HD : (h + 1) * HD].astype(F32)
            part = pl.ds((b % 2) * RB, RB)
            qs[b // 2 * 2 + h, part] = turned(x, cosf[b], sinf[b]).astype(BF)
    share_kv.wait_recv()

    def key_tile(kb):
        return kv2[0, 2 * kb : 2 * kb + 2].reshape(TILE, HD)

    def value_tile(kb):
        return kv2[1, 2 * kb : 2 * kb + 2].reshape(TILE, HD)

    column = lax.broadcasted_iota(jnp.int32, (TILE, TILE), 1)
    row_of = lax.broadcasted_iota(jnp.int32, (TILE, TILE), 0)
    for t in range(TILES):
        first = start[2 * t : 2 * t + 2].reshape(TILE, RB)
        first = jnp.concatenate([first, first], axis=1)

        def forward(h, carry):
            rows = qs[2 * t + h]
            scores = []
            for kb in range(t + 1):
                raw = dot(rows, key_tile(kb), NT)
                allowed = column + kb * TILE >= first
                if kb == t:
                    allowed = allowed & (column <= row_of)
                scores.append(jnp.where(allowed, raw, masked_score))
            peak = functools.reduce(jnp.maximum, scores)
            peak = jnp.max(peak, axis=1, keepdims=True)
            scores = [jnp.exp2((s - peak) * log2_scale) for s in scores]
            total = jnp.sum(functools.reduce(jnp.add, scores), axis=1, keepdims=True)
            share = 1.0 / total
            out = jnp.zeros((TILE, HD), F32)
            for kb in range(t + 1):
                p = scores[kb] * share
                prob[2 * t + h, :, kb * TILE : (kb + 1) * TILE] = p
                out += dot(p.astype(BF), value_tile(kb), NN)
            outs[2 * t : 2 * t + 2, h] = out.astype(BF).reshape(2, RB, HD)
            return carry

        lax.fori_loop(0, 2, forward, 0)

    def fill_out(buffer, at, dest):
        rows = outs[back_slot(dest)]
        for h in range(2):
            buffer[at, :, h * HD : (h + 1) * HD] = rows[h]

    exchange(fill_out, ao_s, ao_r, 2)

    all_moved(ga_s, ga_r, 1).wait_recv()
    for b in range(NB):
        block = ga_r[plan[me * NB + b] >> 3]
        for h in range(2):
            part = pl.ds((b % 2) * RB, RB)
            gas[b // 2 * 2 + h, part] = block[:, h * HD : (h + 1) * HD]

    dkt[...] = jnp.zeros_like(dkt)
    dvt[...] = jnp.zeros_like(dvt)
    for t in range(TILES):
        cosine = cosf[2 * t : 2 * t + 2].reshape(TILE, HD)
        sine = sinf[2 * t : 2 * t + 2].reshape(TILE, HD)

        def backward(h, carry):
            u = 2 * t + h
            upstream = gas[u]
            rows = qs[u]
            out = outs[2 * t : 2 * t + 2, h].reshape(TILE, HD)
            delta = jnp.sum(
                upstream.astype(F32) * out.astype(F32), axis=1, keepdims=True
            )
            dq = jnp.zeros((TILE, HD), F32)
            for kb in range(t + 1):
                cols = slice(kb * TILE, (kb + 1) * TILE)
                p = prob[u, :, cols]
                dp = dot(upstream, value_tile(kb), NT)
                ds = (p * (dp - delta)).astype(BF)
                dq += dot(ds, key_tile(kb), NN)
                dkt[:, cols] += dot(rows, ds, TN)
                dvt[:, cols] += dot(upstream, p.astype(BF), TN)
            dq = turned(dq * inv_scale, cosine, -sine).astype(BF)
            dq_v[2 * t : 2 * t + 2, h] = dq.reshape(2, RB, HD)
            return carry

        lax.fori_loop(0, 2, backward, 0)

    for b in range(NB):
        cols = slice(b * RB, (b + 1) * RB)
        dk = dkt[:, cols].T * inv_scale
        dkv_own[0, b] = turned(dk, cosf[b], -sinf[b]).astype(BF)
        dkv_own[1, b] = dvt[:, cols].T.astype(BF)
    share_dkv = pair_copy(dkv_own.at[1 - core], dkv_in, 1)
    share_dkv.start()

    def fill_dq(buffer, at, dest):
        rows = dq_v[back_slot(dest)]
        for h in range(2):
            buffer[at, :, h * HD : (h + 1) * HD] = rows[h]

    def fill_dkv(buffer, at, dest):
        buffer[at] = dkv_v[back_slot(dest)]

    share_dkv.wait_recv()
    for b in range(NB):
        dkv_v[b] = (dkv_own[core, b].astype(F32) + dkv_in[b].astype(F32)).astype(BF)
    exchange(fill_dkv, dkv_s, dkv_r, 3)

    all_moved(ao_s, ao_r, 2).wait_recv()
    for j in range(NB):
        aoh[j * RB : (j + 1) * RB] = ao_r[homes[j]]
    chunk = SIDE * WROWS
    for c in range(SIDE):
        rows = g_v[:, :, c * chunk : (c + 1) * chunk].reshape(NB * RB, chunk)
        term = dot(aoh[...], rows, TN).T.astype(BF)
        for e in range(SIDE):
            part = term[e * WROWS : (e + 1) * WROWS]
            w_s[0, c, e] = part[:, :HD]
            w_s[1, e, c] = part[:, HD:]

    mine = (my_x, my_y)

    def along(half, step, o, e):
        axis = half if step == 0 else 1 - half
        to = lax.rem(mine[axis] + o, SIDE)
        dest = to * SIDE + my_y if axis == 0 else my_x * SIDE + to
        if step == 0:
            src, dst = w_s.at[half, to, e], w_r.at[half, mine[axis], e]
        else:
            src, dst = w2_s.at[half, to], w2_r.at[half, mine[axis]]
        return pltpu.make_async_remote_copy(
            src_ref=src, dst_ref=dst, send_sem=w_send.at[step, half], recv_sem=w_recv.at[step, half],
            device_id={"dp": dest}, device_id_type=MESH,
        )

    def all_along(half, step):
        stage, landing = ((w_s, w_r), (w2_s, w2_r))[step]
        rest = pl.ds(0, SIDE - 1)
        return pltpu.make_async_remote_copy(
            src_ref=stage.at[half, rest], dst_ref=landing.at[half, rest],
            send_sem=w_send.at[step, half], recv_sem=w_recv.at[step, half],
            device_id={"dp": lax.rem(me + 1, RANKS)}, device_id_type=MESH,
        )

    for e in range(SIDE):
        for o in (1, 3, 2):
            for half in range(2):
                along(half, 0, o, e).start()
    for half in range(2):
        w_r[half, mine[half]] = w_s[half, mine[half]]
    round_of(dq_s, dq_r, 4, 0, fill_dq)

    all_moved(dkv_s, dkv_r, 3).wait_recv()
    for j in range(NB):
        zk[core, zed, j] = dkv_r[homes[j]]
    z_copies = []
    for o in range(1, 4):
        copy = pltpu.make_async_remote_copy(
            src_ref=zk.at[core, zed], dst_ref=zk.at[core, zed],
            send_sem=z_send.at[o - 1], recv_sem=z_recv.at[o - 1],
            device_id={"tensor": lax.rem(zed + o, 4) * 2 + core}, device_id_type=MESH,
        )
        copy.start()
        z_copies.append(copy)

    for half in range(2):
        all_along(half, 0).wait_recv()
    for half in range(2):
        for e in range(SIDE):
            total = jnp.zeros((WROWS, HD), F32)
            for r in range(SIDE):
                total += w_r[half, r, e].astype(F32)
            w2_s[half, e] = total.astype(BF)
    for o in (1, 3, 2):
        for half in range(2):
            along(half, 1, o, 0).start()
    for half in range(2):
        w2_r[half, mine[1 - half]] = w2_s[half, mine[1 - half]]
    round_of(dq_s, dq_r, 4, 1, fill_dq)

    for copy in z_copies:
        copy.wait_recv()
    share_z = pair_copy(zk.at[core], zk.at[core], 2)
    share_z.start()
    share_z.wait_recv()
    copies = []
    for k, target in enumerate((gk_hbm, gv_hbm)):
        for z in range(KV):
            copy = pltpu.make_async_copy(
                zk.at[k, z], target.at[:, :, z * HD : (z + 1) * HD], out_sem.at[1 + 4 * k + z]
            )
            copy.start()
            copies.append(copy)

    for half in range(2):
        all_along(half, 1).wait_recv()
    for half in range(2):
        total = jnp.zeros((WROWS, HD), F32)
        for r in range(SIDE):
            total += w2_r[half, r].astype(F32)
        gw_v[:, half * HD : (half + 1) * HD] = total * (1.0 / RANKS)
    gw_out = pltpu.make_async_copy(gw_v, gw_hbm, out_sem.at[9])
    gw_out.start()

    all_moved(dq_s, dq_r, 4).wait_recv()
    for j in range(NB):
        q_v[j] = dq_r[homes[j]]
    gq_out = pltpu.make_async_copy(q_v, gq_hbm, out_sem.at[0])
    gq_out.start()

    for kind, (stage, landing) in enumerate(
        ((q_s, q_r), (ga_s, ga_r), (ao_s, ao_r), (dkv_s, dkv_r), (dq_s, dq_r), (kv_s, kv_r))
    ):
        all_moved(stage, landing, kind).wait_send()
    for half in range(2):
        for step in range(2):
            all_along(half, step).wait_send()
    share_kv.wait_send()
    share_dkv.wait_send()
    share_z.wait_send()
    for copy in z_copies:
        copy.wait_send()
    gq_out.wait()
    for copy in copies:
        copy.wait()
    gw_out.wait()


def hand_on(*refs):
    source, target, held, sems = refs[:4], refs[4:8], refs[8:12], refs[12]
    parts = []
    for k in range(4):
        half = source[k].shape[0] // 2
        for h in range(2):
            part = pl.ds(h * half, half)
            sem = sems.at[2 * k + h]
            parts.append(
                (
                    pltpu.make_async_copy(source[k].at[part], held[k].at[part], sem),
                    pltpu.make_async_copy(held[k].at[part], target[k].at[part], sem),
                )
            )
    for load, store in parts:
        load.start()
    for load, store in parts:
        load.wait()
        store.start()
    for load, store in parts:
        store.wait()


def local(query, key, value, grad_out, out_weight, plan, segments):
    blocked = (NB, RB)
    half = yarn_frequencies(HD)
    freq = np.tile(np.concatenate([half, half]), (8, 1)).astype(np.float32)
    hbm = pl.BlockSpec(memory_space=pl.ANY)
    vmem = pl.BlockSpec(memory_space=pltpu.VMEM)
    V = pltpu.VMEM
    dma = pltpu.SemaphoreType.DMA
    rows = NB * RB
    gq, gk, gv, gw = pl.pallas_call(
        kernel,
        out_shape=(
            jax.ShapeDtypeStruct(blocked + (COLS,), BF),
            jax.ShapeDtypeStruct(blocked + (KV * HD,), BF),
            jax.ShapeDtypeStruct(blocked + (KV * HD,), BF),
            jax.ShapeDtypeStruct((WROWS, COLS), F32),
        ),
        in_specs=[pl.BlockSpec(memory_space=pltpu.SMEM), vmem, vmem] + [hbm] * 5,
        out_specs=(hbm,) * 4,
        scratch_shapes=[
            V(blocked + (COLS,), BF),
            V(blocked + (HD,), BF),
            V(blocked + (D,), BF),
            V((D, COLS), BF),
            V((RANKS, RB, COLS), BF),
            V((RANKS, RB, COLS), BF),
            V((RANKS, RB, HD), BF),
            V((RANKS, RB, HD), BF),
            V(blocked + (COLS,), BF),
            V((RANKS, RB, COLS), BF),
            V((RANKS, RB, COLS), BF),
            V((2,) + blocked + (HD,), BF),
            V((2 * TILES, TILE, HD), BF),
            V((2 * TILES, TILE, HD), BF),
            V((NB, 2, RB, HD), BF),
            V((2 * TILES, TILE, rows), F32),
            V((RANKS, RB, COLS), BF),
            V((RANKS, RB, COLS), BF),
            V((NB, 2, RB, HD), BF),
            V((RANKS, RB, COLS), BF),
            V((RANKS, RB, COLS), BF),
            V((HD, rows), F32),
            V((HD, rows), F32),
            V((2,) + blocked + (HD,), BF),
            V(blocked + (HD,), BF),
            V(blocked + (HD,), BF),
            V((RANKS, RB, HD), BF),
            V((RANKS, RB, HD), BF),
            V((2, SIDE, SIDE, WROWS, HD), BF),
            V((2, SIDE, SIDE, WROWS, HD), BF),
            V((2, SIDE, WROWS, HD), BF),
            V((2, SIDE, WROWS, HD), BF),
            V((2, KV) + blocked + (HD,), BF),
            V((rows, COLS), BF),
            V((WROWS, COLS), F32),
            V(blocked + (HD,), F32),
            V(blocked + (HD,), F32),
            V(blocked + (RB,), jnp.int32),
            dma((3,)),
            dma((TILES,)),
            dma((6,)),
            dma((6,)),
            dma((3,)),
            dma((3,)),
            dma((3,)),
            dma((3,)),
            dma((2, 2)),
            dma((2, 2)),
            dma((10,)),
        ],
        compiler_params=pltpu.CompilerParams(
            collective_id=0, has_side_effects=True, vmem_limit_bytes=60 * 2**20
        ),
        cost_estimate=pl.CostEstimate(
            flops=7 * 10**9, bytes_accessed=14 * 2**20, transcendentals=2 * 10**6
        ),
    )(
        plan,
        segments.reshape(NB, RB),
        freq,
        query.reshape(blocked + (COLS,)),
        key.reshape(blocked + (KV * HD,)),
        value.reshape(blocked + (KV * HD,)),
        grad_out.reshape(blocked + (D,)),
        out_weight,
    )
    gq, gk, gv, gw = pl.pallas_call(
        hand_on,
        out_shape=tuple(jax.ShapeDtypeStruct(x.shape, x.dtype) for x in (gq, gk, gv, gw)),
        in_specs=[hbm] * 4,
        out_specs=(hbm,) * 4,
        scratch_shapes=[V(x.shape, x.dtype) for x in (gq, gk, gv, gw)] + [dma((8,))],
    )(gq, gk, gv, gw)
    return (
        gq.reshape(rows, COLS),
        gk.reshape(rows, KV * HD),
        gv.reshape(rows, KV * HD),
        gw,
    )


def solution(mesh):
    in_specs = (
        P("dp", "tensor"),
        P("dp", None),
        P("dp", None),
        P("dp", None),
        P(None, "tensor"),
        P(),
        P("dp"),
    )
    out_specs = (P("dp", "tensor"), P("dp", None), P("dp", None), P("dp", "tensor"))
    return jax.shard_map(local, mesh=mesh, in_specs=in_specs, out_specs=out_specs, check_vma=False)
```

```python
import functools
import math

import jax
import jax.numpy as jnp
import numpy as np
from jax import lax
from jax.experimental import pallas as pl
from jax.experimental.pallas import tpu as pltpu
from jax.sharding import PartitionSpec as P

D = 3584
KV = 4
HD = 128
HEADS = 16
RB = 128
NB = 8
RANKS = 16
LANES = 8
COLS = 256
TILE = 256
TILES = NB * RB // TILE
WROWS = D // RANKS
SIDE = 4
ORDER = (
    (1, 0), (0, 1), (3, 3), (2, 0), (0, 3), (1, 1), (3, 0), (0, 2),
    (1, 3), (3, 1), (2, 2), (1, 2), (2, 3), (3, 2), (2, 1),
)
DX = sum(dx << (2 * i) for i, (dx, dy) in enumerate(ORDER))
DY = sum(dy << (2 * i) for i, (dx, dy) in enumerate(ORDER))

rope_base = 1000000.0
yarn_factor = 4.0
yarn_context = 32768.0
beta_fast = 32.0
beta_slow = 1.0
masked_score = -1e30
MESH = pl.DeviceIdType.MESH
BF = jnp.bfloat16
F32 = jnp.float32


def yarn_frequencies(head_size):
    half_size = head_size // 2

    def correction(rotations):
        return (
            head_size
            * math.log(yarn_context / (rotations * 2.0 * math.pi))
            / (2.0 * math.log(rope_base))
        )

    lower_bound = max(math.floor(correction(beta_fast)), 0)
    upper_bound = min(math.ceil(correction(beta_slow)), head_size - 1)
    ramp_span = max(upper_bound - lower_bound, 0.001)
    row_index = np.arange(half_size).astype(np.float64)
    extrap_freq = rope_base ** (-2.0 * row_index / head_size)
    interp_freq = extrap_freq / yarn_factor
    ramp_weight = np.clip((row_index - lower_bound) / ramp_span, 0.0, 1.0)
    return interp_freq * ramp_weight + extrap_freq * (1.0 - ramp_weight)


def dot(a, b, dims):
    return lax.dot_general(a, b, (dims, ((), ())), preferred_element_type=F32)


NN = ((1,), (0,))
NT = ((1,), (1,))
TN = ((0,), (0,))


def kernel(
    plan, seg, freq, q_hbm, k_hbm, v_hbm, g_hbm, w_hbm,
    gq_hbm, gk_hbm, gv_hbm, gw_hbm,
    q_v, kv_v, g_v, w_v, q_s, q_r, kv_s, kv_r, ga_v, ga_s, ga_r, kv2, qs, gas, outs, prob,
    ao_s, ao_r, dq_v, dq_s, dq_r, dkt, dvt, dkv_own, dkv_in, dkv_v, dkv_s, dkv_r,
    w_s, w_r, wn_r, wb_s, w2_s, w2_r, zk, aoh, gw_v, cosf, sinf, start,
    in_sem, g_sem, send_sem, recv_sem, pair_send, pair_recv, z_send, z_recv, w_send, w_recv, w2_send, w2_recv, out_sem,
):
    me = lax.axis_index("dp")
    lane = lax.axis_index("tensor")
    core = lax.rem(lane, 2)
    zed = lane // 2
    partner = lane + 1 - 2 * core
    my_x = me // SIDE
    my_y = lax.rem(me, SIDE)
    inv_scale = 1.0 / math.sqrt(HD)
    log2_scale = inv_scale * math.log2(math.e)

    barrier = pltpu.get_barrier_semaphore()

    def greet(o, carry):
        pl.semaphore_signal(
            barrier, inc=1, device_id={"dp": lax.rem(me + o, RANKS)}, device_id_type=MESH
        )
        return carry

    lax.fori_loop(1, RANKS, greet, 0)
    pl.semaphore_signal(barrier, inc=1, device_id={"tensor": partner}, device_id_type=MESH)
    for o in range(1, 4):
        peer = lax.rem(zed + o, 4) * 2 + core
        pl.semaphore_signal(barrier, inc=1, device_id={"tensor": peer}, device_id_type=MESH)

    q_in = pltpu.make_async_copy(q_hbm, q_v, in_sem.at[0])
    q_in.start()
    head_cols = pl.ds(pl.multiple_of(zed * HD, HD), HD)
    k_in = pltpu.make_async_copy(k_hbm.at[:, :, head_cols], kv_v, in_sem.at[1])
    v_in = pltpu.make_async_copy(v_hbm.at[:, :, head_cols], kv_v, in_sem.at[1])
    pl.when(core == 0)(k_in.start)
    pl.when(core == 1)(v_in.start)
    w_in = pltpu.make_async_copy(w_hbm, w_v, in_sem.at[2])
    w_in.start()
    g_in = [
        pltpu.make_async_copy(
            g_hbm.at[pl.ds(2 * t, 2)], g_v.at[pl.ds(2 * t, 2)], g_sem.at[t]
        )
        for t in range(TILES)
    ]
    for copy in g_in:
        copy.start()

    def send_slot(dest):
        slot = jnp.int32(0)
        for b in range(NB):
            source = plan[dest * NB + b]
            slot = jnp.where((source >> 3) == me, source & 7, slot)
        return slot

    def back_slot(dest):
        slot = jnp.int32(0)
        for b in range(NB):
            slot = jnp.where((plan[me * NB + b] >> 3) == dest, b, slot)
        return slot

    def moved(stage, landing, kind, dest, h):
        return pltpu.make_async_remote_copy(
            src_ref=stage.at[dest, pl.ds(64 * h, 64)],
            dst_ref=landing.at[me, pl.ds(64 * h, 64)],
            send_sem=send_sem.at[kind],
            recv_sem=recv_sem.at[kind],
            device_id={"dp": dest},
            device_id_type=MESH,
        )

    def all_moved(stage, landing, kind):
        rest = pl.ds(0, RANKS - 1)
        return pltpu.make_async_remote_copy(
            src_ref=stage.at[rest],
            dst_ref=landing.at[rest],
            send_sem=send_sem.at[kind],
            recv_sem=recv_sem.at[kind],
            device_id={"dp": lax.rem(me + 1, RANKS)},
            device_id_type=MESH,
        )

    def round_of(stage, landing, kind, half, fill):
        def one(o, carry):
            dxs, dys = carry
            x = lax.rem(my_x + lax.rem(dxs, SIDE), SIDE)
            y = lax.rem(my_y + lax.rem(dys, SIDE), SIDE)
            dest = x * SIDE + y
            if half == 0:
                fill(stage, dest, dest)
            moved(stage, landing, kind, dest, half).start()
            return dxs // SIDE, dys // SIDE

        lax.fori_loop(1, RANKS, one, (DX + core * (DY - DX), DY + core * (DX - DY)))
        if half == 0:
            fill(landing, me, me)

    def exchange(fill, stage, landing, kind):
        for half in range(2):
            round_of(stage, landing, kind, half, fill)

    pl.when(core == 0)(k_in.wait)
    pl.when(core == 1)(v_in.wait)
    pl.semaphore_wait(barrier, RANKS - 1 + 4)

    def fill_kv(buffer, at, dest):
        buffer[at] = kv_v[send_slot(dest)]

    exchange(fill_kv, kv_s, kv_r, 5)

    q_in.wait()

    def fill_q(buffer, at, dest):
        buffer[at] = q_v[send_slot(dest)]

    exchange(fill_q, q_s, q_r, 0)

    w_in.wait()
    for t in range(TILES):
        g_in[t].wait()
    def project(t, carry):
        rows = pl.ds(2 * t, 2)
        product = dot(g_v[rows].reshape(TILE, D), w_v[...], NN)
        ga_v[rows] = product.astype(BF).reshape(2, RB, COLS)
        return carry

    lax.fori_loop(0, TILES, project, 0)

    def fill_ga(buffer, at, dest):
        buffer[at] = ga_v[send_slot(dest)]

    exchange(fill_ga, ga_s, ga_r, 1)

    factor = 0.1 * math.log(yarn_factor) + 1.0
    sign = jnp.where(lax.broadcasted_iota(jnp.int32, (1, RB), 1) < HD // 2, -factor, factor)
    for b in range(NB):
        mine = jnp.broadcast_to(seg[b : b + 1, :], (RB, RB)).T
        smaller = jnp.zeros((RB, RB), jnp.int32)
        for other in range(b + 1):
            smaller += jnp.where(seg[other : other + 1, :] < mine, 1, 0)
        first = jnp.sum(smaller, axis=1, keepdims=True)
        start[b] = jnp.broadcast_to(first, (RB, RB))

    def tables(b, carry):
        row = b * RB + lax.broadcasted_iota(jnp.int32, (RB, RB), 0)
        angle = (row - start[b]).astype(F32) * freq[0:1, :]
        cosf[b] = jnp.cos(angle) * factor
        sinf[b] = jnp.sin(angle) * sign
        return carry

    lax.fori_loop(0, NB, tables, 0)

    def find(g, carry):
        source = plan[g] - me * NB
        return tuple(jnp.where(source == j, g // NB, carry[j]) for j in range(NB))

    homes = lax.fori_loop(0, RANKS * NB, find, (jnp.int32(0),) * NB)

    def turned(x, cosine, sine):
        return x * cosine + pltpu.roll(x, HD // 2, 1) * sine

    def pair_copy(src, dst, i):
        return pltpu.make_async_remote_copy(
            src_ref=src, dst_ref=dst, send_sem=pair_send.at[i], recv_sem=pair_recv.at[i],
            device_id={"tensor": partner}, device_id_type=MESH,
        )

    all_moved(kv_s, kv_r, 5).wait_recv()
    is_key = (core == 0).astype(F32)

    def arrive_kv(b, carry):
        origin = plan[me * NB + b] >> 3
        x = kv_r[origin].astype(F32)
        cosine = cosf[b] * is_key + (1.0 - is_key)
        kv2[core, b] = turned(x, cosine, sinf[b] * is_key).astype(BF)
        return carry

    lax.fori_loop(0, NB, arrive_kv, 0)
    share_kv = pair_copy(kv2.at[core], kv2.at[core], 0)
    share_kv.start()

    all_moved(q_s, q_r, 0).wait_recv()
    for b in range(NB):
        block = q_r[plan[me * NB + b] >> 3]
        for h in range(2):
            x = block[:, h * HD : (h + 1) * HD].astype(F32)
            part = pl.ds((b % 2) * RB, RB)
            qs[b // 2 * 2 + h, part] = turned(x, cosf[b], sinf[b]).astype(BF)
    share_kv.wait_recv()

    def key_tile(kb):
        return kv2[0, 2 * kb : 2 * kb + 2].reshape(TILE, HD)

    def value_tile(kb):
        return kv2[1, 2 * kb : 2 * kb + 2].reshape(TILE, HD)

    column = lax.broadcasted_iota(jnp.int32, (TILE, TILE), 1)
    row_of = lax.broadcasted_iota(jnp.int32, (TILE, TILE), 0)
    for t in range(TILES):
        first = start[2 * t : 2 * t + 2].reshape(TILE, RB)
        first = jnp.concatenate([first, first], axis=1)

        def forward(h, carry):
            rows = qs[2 * t + h]
            scores = []
            for kb in range(t + 1):
                raw = dot(rows, key_tile(kb), NT)
                allowed = column + kb * TILE >= first
                if kb == t:
                    allowed = allowed & (column <= row_of)
                scores.append(jnp.where(allowed, raw, masked_score))
            peak = functools.reduce(jnp.maximum, scores)
            peak = jnp.max(peak, axis=1, keepdims=True)
            scores = [jnp.exp2((s - peak) * log2_scale) for s in scores]
            total = jnp.sum(functools.reduce(jnp.add, scores), axis=1, keepdims=True)
            share = 1.0 / total
            out = jnp.zeros((TILE, HD), F32)
            for kb in range(t + 1):
                p = scores[kb] * share
                prob[2 * t + h, :, kb * TILE : (kb + 1) * TILE] = p
                out += dot(p.astype(BF), value_tile(kb), NN)
            outs[2 * t : 2 * t + 2, h] = out.astype(BF).reshape(2, RB, HD)
            return carry

        lax.fori_loop(0, 2, forward, 0)

    def fill_out(buffer, at, dest):
        rows = outs[back_slot(dest)]
        for h in range(2):
            buffer[at, :, h * HD : (h + 1) * HD] = rows[h]

    exchange(fill_out, ao_s, ao_r, 2)

    all_moved(ga_s, ga_r, 1).wait_recv()
    for b in range(NB):
        block = ga_r[plan[me * NB + b] >> 3]
        for h in range(2):
            part = pl.ds((b % 2) * RB, RB)
            gas[b // 2 * 2 + h, part] = block[:, h * HD : (h + 1) * HD]

    dkt[...] = jnp.zeros_like(dkt)
    dvt[...] = jnp.zeros_like(dvt)
    for t in range(TILES):
        cosine = cosf[2 * t : 2 * t + 2].reshape(TILE, HD)
        sine = sinf[2 * t : 2 * t + 2].reshape(TILE, HD)

        def backward(h, carry):
            u = 2 * t + h
            upstream = gas[u]
            rows = qs[u]
            out = outs[2 * t : 2 * t + 2, h].reshape(TILE, HD)
            delta = jnp.sum(
                upstream.astype(F32) * out.astype(F32), axis=1, keepdims=True
            )
            dq = jnp.zeros((TILE, HD), F32)
            for kb in range(t + 1):
                cols = slice(kb * TILE, (kb + 1) * TILE)
                p = prob[u, :, cols]
                dp = dot(upstream, value_tile(kb), NT)
                ds = (p * (dp - delta)).astype(BF)
                dq += dot(ds, key_tile(kb), NN)
                dkt[:, cols] += dot(rows, ds, TN)
                dvt[:, cols] += dot(upstream, p.astype(BF), TN)
            dq = turned(dq * inv_scale, cosine, -sine).astype(BF)
            dq_v[2 * t : 2 * t + 2, h] = dq.reshape(2, RB, HD)
            return carry

        lax.fori_loop(0, 2, backward, 0)

    for b in range(NB):
        cols = slice(b * RB, (b + 1) * RB)
        dk = dkt[:, cols].T * inv_scale
        dkv_own[0, b] = turned(dk, cosf[b], -sinf[b]).astype(BF)
        dkv_own[1, b] = dvt[:, cols].T.astype(BF)
    share_dkv = pair_copy(dkv_own.at[1 - core], dkv_in, 1)
    share_dkv.start()

    def fill_dq(buffer, at, dest):
        rows = dq_v[back_slot(dest)]
        for h in range(2):
            buffer[at, :, h * HD : (h + 1) * HD] = rows[h]

    def fill_dkv(buffer, at, dest):
        buffer[at] = dkv_v[back_slot(dest)]

    share_dkv.wait_recv()
    for b in range(NB):
        dkv_v[b] = (dkv_own[core, b].astype(F32) + dkv_in[b].astype(F32)).astype(BF)
    exchange(fill_dkv, dkv_s, dkv_r, 3)

    all_moved(ao_s, ao_r, 2).wait_recv()
    for j in range(NB):
        aoh[j * RB : (j + 1) * RB] = ao_r[homes[j]]
    chunk = SIDE * WROWS
    for c in range(SIDE):
        rows = g_v[:, :, c * chunk : (c + 1) * chunk].reshape(NB * RB, chunk)
        term = dot(aoh[...], rows, TN).T.astype(BF)
        for e in range(SIDE):
            part = term[e * WROWS : (e + 1) * WROWS]
            w_s[0, c, e] = part[:, :HD]
            w_s[1, e, c] = part[:, HD:]

    mine = (my_x, my_y)

    def beside(axis, by):
        to = lax.rem(mine[axis] + by, SIDE)
        return to, (to * SIDE + my_y if axis == 0 else my_x * SIDE + to)

    def near(kind, half, way):
        to, dest = beside(half, (1, SIDE - 1)[way])
        relayed, plain = pl.ds(2 * way, 2), pl.ds(2 - 2 * way, 2)
        src, dst = (
            (w_s.at[half, lax.rem(mine[half] + 2, SIDE), relayed], w_r.at[half, way]),
            (w_s.at[half, to, plain], wn_r.at[half, way, plain]),
            (wb_s.at[half, way], wn_r.at[half, way, relayed]),
        )[kind]
        return pltpu.make_async_remote_copy(
            src_ref=src, dst_ref=dst,
            send_sem=w_send.at[kind, half, way], recv_sem=w_recv.at[kind, half, way],
            device_id={"dp": dest}, device_id_type=MESH,
        )

    def last(half, o):
        to, dest = beside(1 - half, o)
        return pltpu.make_async_remote_copy(
            src_ref=w2_s.at[half, to], dst_ref=w2_r.at[half, mine[1 - half]],
            send_sem=w2_send.at[half, o - 1], recv_sem=w2_recv.at[half, o - 1],
            device_id={"dp": dest}, device_id_type=MESH,
        )

    ways = [(half, way) for way in range(2) for half in range(2)]
    near_copies = [[near(kind, half, way) for half, way in ways] for kind in range(3)]
    last_copies = [last(half, o) for o in (1, 3, 2) for half in range(2)]
    for kind in range(2):
        for copy in near_copies[kind]:
            copy.start()
    for i, (half, way) in enumerate(ways):
        to, dest = beside(half, (1, SIDE - 1)[way])
        near_copies[0][i].wait_recv()
        both = w_r[half, way].astype(F32) + w_s[half, to, 2 * way : 2 * way + 2].astype(F32)
        wb_s[half, way] = both.astype(BF)
        near_copies[2][i].start()
    round_of(dq_s, dq_r, 4, 0, fill_dq)

    all_moved(dkv_s, dkv_r, 3).wait_recv()
    for j in range(NB):
        zk[core, zed, j] = dkv_r[homes[j]]
    z_copies = []
    for o in range(1, 4):
        copy = pltpu.make_async_remote_copy(
            src_ref=zk.at[core, zed], dst_ref=zk.at[core, zed],
            send_sem=z_send.at[o - 1], recv_sem=z_recv.at[o - 1],
            device_id={"tensor": lax.rem(zed + o, 4) * 2 + core}, device_id_type=MESH,
        )
        copy.start()
        z_copies.append(copy)

    for copy in near_copies[1] + near_copies[2]:
        copy.wait_recv()
    for half in range(2):
        for e in range(SIDE):
            total = w_s[half, mine[half], e].astype(F32)
            for way in range(2):
                total += wn_r[half, way, e].astype(F32)
            w2_s[half, e] = total.astype(BF)
    for copy in last_copies:
        copy.start()
    for half in range(2):
        w2_r[half, mine[1 - half]] = w2_s[half, mine[1 - half]]
    round_of(dq_s, dq_r, 4, 1, fill_dq)

    for copy in z_copies:
        copy.wait_recv()
    share_z = pair_copy(zk.at[core], zk.at[core], 2)
    share_z.start()
    share_z.wait_recv()
    copies = []
    for k, target in enumerate((gk_hbm, gv_hbm)):
        for z in range(KV):
            copy = pltpu.make_async_copy(
                zk.at[k, z], target.at[:, :, z * HD : (z + 1) * HD], out_sem.at[1 + 4 * k + z]
            )
            copy.start()
            copies.append(copy)

    for copy in last_copies:
        copy.wait_recv()
    for half in range(2):
        total = jnp.zeros((WROWS, HD), F32)
        for r in range(SIDE):
            total += w2_r[half, r].astype(F32)
        gw_v[:, half * HD : (half + 1) * HD] = total * (1.0 / RANKS)
    gw_out = pltpu.make_async_copy(gw_v, gw_hbm, out_sem.at[9])
    gw_out.start()

    all_moved(dq_s, dq_r, 4).wait_recv()
    for j in range(NB):
        q_v[j] = dq_r[homes[j]]
    gq_out = pltpu.make_async_copy(q_v, gq_hbm, out_sem.at[0])
    gq_out.start()

    for kind, (stage, landing) in enumerate(
        ((q_s, q_r), (ga_s, ga_r), (ao_s, ao_r), (dkv_s, dkv_r), (dq_s, dq_r), (kv_s, kv_r))
    ):
        all_moved(stage, landing, kind).wait_send()
    for copy in near_copies[0] + near_copies[1] + near_copies[2] + last_copies:
        copy.wait_send()
    share_kv.wait_send()
    share_dkv.wait_send()
    share_z.wait_send()
    for copy in z_copies:
        copy.wait_send()
    gq_out.wait()
    for copy in copies:
        copy.wait()
    gw_out.wait()


def hand_on(*refs):
    source, target, held, sems = refs[:4], refs[4:8], refs[8:12], refs[12]
    parts = []
    for k in range(4):
        half = source[k].shape[0] // 2
        for h in range(2):
            part = pl.ds(h * half, half)
            sem = sems.at[2 * k + h]
            parts.append(
                (
                    pltpu.make_async_copy(source[k].at[part], held[k].at[part], sem),
                    pltpu.make_async_copy(held[k].at[part], target[k].at[part], sem),
                )
            )
    for load, store in parts:
        load.start()
    for load, store in parts:
        load.wait()
        store.start()
    for load, store in parts:
        store.wait()


def local(query, key, value, grad_out, out_weight, plan, segments):
    blocked = (NB, RB)
    half = yarn_frequencies(HD)
    freq = np.tile(np.concatenate([half, half]), (8, 1)).astype(np.float32)
    hbm = pl.BlockSpec(memory_space=pl.ANY)
    vmem = pl.BlockSpec(memory_space=pltpu.VMEM)
    V = pltpu.VMEM
    dma = pltpu.SemaphoreType.DMA
    rows = NB * RB
    gq, gk, gv, gw = pl.pallas_call(
        kernel,
        out_shape=(
            jax.ShapeDtypeStruct(blocked + (COLS,), BF),
            jax.ShapeDtypeStruct(blocked + (KV * HD,), BF),
            jax.ShapeDtypeStruct(blocked + (KV * HD,), BF),
            jax.ShapeDtypeStruct((WROWS, COLS), F32),
        ),
        in_specs=[pl.BlockSpec(memory_space=pltpu.SMEM), vmem, vmem] + [hbm] * 5,
        out_specs=(hbm,) * 4,
        scratch_shapes=[
            V(blocked + (COLS,), BF),
            V(blocked + (HD,), BF),
            V(blocked + (D,), BF),
            V((D, COLS), BF),
            V((RANKS, RB, COLS), BF),
            V((RANKS, RB, COLS), BF),
            V((RANKS, RB, HD), BF),
            V((RANKS, RB, HD), BF),
            V(blocked + (COLS,), BF),
            V((RANKS, RB, COLS), BF),
            V((RANKS, RB, COLS), BF),
            V((2,) + blocked + (HD,), BF),
            V((2 * TILES, TILE, HD), BF),
            V((2 * TILES, TILE, HD), BF),
            V((NB, 2, RB, HD), BF),
            V((2 * TILES, TILE, rows), F32),
            V((RANKS, RB, COLS), BF),
            V((RANKS, RB, COLS), BF),
            V((NB, 2, RB, HD), BF),
            V((RANKS, RB, COLS), BF),
            V((RANKS, RB, COLS), BF),
            V((HD, rows), F32),
            V((HD, rows), F32),
            V((2,) + blocked + (HD,), BF),
            V(blocked + (HD,), BF),
            V(blocked + (HD,), BF),
            V((RANKS, RB, HD), BF),
            V((RANKS, RB, HD), BF),
            V((2, SIDE, SIDE, WROWS, HD), BF),
            V((2, 2, 2, WROWS, HD), BF),
            V((2, 2, SIDE, WROWS, HD), BF),
            V((2, 2, 2, WROWS, HD), BF),
            V((2, SIDE, WROWS, HD), BF),
            V((2, SIDE, WROWS, HD), BF),
            V((2, KV) + blocked + (HD,), BF),
            V((rows, COLS), BF),
            V((WROWS, COLS), F32),
            V(blocked + (HD,), F32),
            V(blocked + (HD,), F32),
            V(blocked + (RB,), jnp.int32),
            dma((3,)),
            dma((TILES,)),
            dma((6,)),
            dma((6,)),
            dma((3,)),
            dma((3,)),
            dma((3,)),
            dma((3,)),
            dma((3, 2, 2)),
            dma((3, 2, 2)),
            dma((2, 3)),
            dma((2, 3)),
            dma((10,)),
        ],
        compiler_params=pltpu.CompilerParams(
            collective_id=0, has_side_effects=True, vmem_limit_bytes=60 * 2**20
        ),
        cost_estimate=pl.CostEstimate(
            flops=7 * 10**9, bytes_accessed=14 * 2**20, transcendentals=2 * 10**6
        ),
    )(
        plan,
        segments.reshape(NB, RB),
        freq,
        query.reshape(blocked + (COLS,)),
        key.reshape(blocked + (KV * HD,)),
        value.reshape(blocked + (KV * HD,)),
        grad_out.reshape(blocked + (D,)),
        out_weight,
    )
    gq, gk, gv, gw = pl.pallas_call(
        hand_on,
        out_shape=tuple(jax.ShapeDtypeStruct(x.shape, x.dtype) for x in (gq, gk, gv, gw)),
        in_specs=[hbm] * 4,
        out_specs=(hbm,) * 4,
        scratch_shapes=[V(x.shape, x.dtype) for x in (gq, gk, gv, gw)] + [dma((8,))],
    )(gq, gk, gv, gw)
    return (
        gq.reshape(rows, COLS),
        gk.reshape(rows, KV * HD),
        gv.reshape(rows, KV * HD),
        gw,
    )


def solution(mesh):
    in_specs = (
        P("dp", "tensor"),
        P("dp", None),
        P("dp", None),
        P("dp", None),
        P(None, "tensor"),
        P(),
        P("dp"),
    )
    out_specs = (P("dp", "tensor"), P("dp", None), P("dp", None), P("dp", "tensor"))
    return jax.shard_map(local, mesh=mesh, in_specs=in_specs, out_specs=out_specs, check_vma=False)
```

```python
import functools
import math

import jax
import jax.numpy as jnp
import numpy as np
from jax import lax
from jax.experimental import pallas as pl
from jax.experimental.pallas import tpu as pltpu
from jax.sharding import PartitionSpec as P

D = 3584
KV = 4
HD = 128
HEADS = 16
RB = 128
NB = 8
RANKS = 16
LANES = 8
COLS = 256
TILE = 256
TILES = NB * RB // TILE
WROWS = D // RANKS
SIDE = 4
ORDER = (
    (2, 2), (1, 0), (0, 1), (1, 2), (3, 0), (0, 3), (2, 1), (1, 1),
    (3, 2), (2, 0), (3, 3), (2, 3), (0, 2), (1, 3), (3, 1),
)
DX = sum(dx << (2 * i) for i, (dx, dy) in enumerate(ORDER))
DY = sum(dy << (2 * i) for i, (dx, dy) in enumerate(ORDER))

rope_base = 1000000.0
yarn_factor = 4.0
yarn_context = 32768.0
beta_fast = 32.0
beta_slow = 1.0
masked_score = -1e30
MESH = pl.DeviceIdType.MESH
BF = jnp.bfloat16
F32 = jnp.float32


def yarn_frequencies(head_size):
    half_size = head_size // 2

    def correction(rotations):
        return (
            head_size
            * math.log(yarn_context / (rotations * 2.0 * math.pi))
            / (2.0 * math.log(rope_base))
        )

    lower_bound = max(math.floor(correction(beta_fast)), 0)
    upper_bound = min(math.ceil(correction(beta_slow)), head_size - 1)
    ramp_span = max(upper_bound - lower_bound, 0.001)
    row_index = np.arange(half_size).astype(np.float64)
    extrap_freq = rope_base ** (-2.0 * row_index / head_size)
    interp_freq = extrap_freq / yarn_factor
    ramp_weight = np.clip((row_index - lower_bound) / ramp_span, 0.0, 1.0)
    return interp_freq * ramp_weight + extrap_freq * (1.0 - ramp_weight)


def dot(a, b, dims):
    return lax.dot_general(a, b, (dims, ((), ())), preferred_element_type=F32)


NN = ((1,), (0,))
NT = ((1,), (1,))
TN = ((0,), (0,))


def kernel(
    plan, seg, freq, q_hbm, k_hbm, v_hbm, g_hbm, w_hbm,
    gq_hbm, gk_hbm, gv_hbm, gw_hbm,
    q_v, kv_v, g_v, w_v, q_s, q_r, kv_s, kv_r, ga_v, ga_s, ga_r, kv2, qs, gas, outs, prob,
    ao_s, ao_r, dq_v, dq_s, dq_r, dkt, dvt, dkv_own, dkv_in, dkv_v, dkv_s, dkv_r,
    w_s, w_r, wn_r, wb_s, w2_s, w2_r, zk, aoh, gw_v, cosf, sinf, start,
    in_sem, g_sem, send_sem, recv_sem, pair_send, pair_recv, z_send, z_recv, w_send, w_recv, w2_send, w2_recv, out_sem,
):
    me = lax.axis_index("dp")
    lane = lax.axis_index("tensor")
    core = lax.rem(lane, 2)
    zed = lane // 2
    partner = lane + 1 - 2 * core
    my_x = me // SIDE
    my_y = lax.rem(me, SIDE)
    inv_scale = 1.0 / math.sqrt(HD)
    log2_scale = inv_scale * math.log2(math.e)

    barrier = pltpu.get_barrier_semaphore()

    def greet(o, carry):
        pl.semaphore_signal(
            barrier, inc=1, device_id={"dp": lax.rem(me + o, RANKS)}, device_id_type=MESH
        )
        return carry

    lax.fori_loop(1, RANKS, greet, 0)
    pl.semaphore_signal(barrier, inc=1, device_id={"tensor": partner}, device_id_type=MESH)
    for o in range(1, 4):
        peer = lax.rem(zed + o, 4) * 2 + core
        pl.semaphore_signal(barrier, inc=1, device_id={"tensor": peer}, device_id_type=MESH)

    q_in = pltpu.make_async_copy(q_hbm, q_v, in_sem.at[0])
    q_in.start()
    head_cols = pl.ds(pl.multiple_of(zed * HD, HD), HD)
    k_in = pltpu.make_async_copy(k_hbm.at[:, :, head_cols], kv_v, in_sem.at[1])
    v_in = pltpu.make_async_copy(v_hbm.at[:, :, head_cols], kv_v, in_sem.at[1])
    pl.when(core == 0)(k_in.start)
    pl.when(core == 1)(v_in.start)
    w_in = pltpu.make_async_copy(w_hbm, w_v, in_sem.at[2])
    w_in.start()
    g_in = [
        pltpu.make_async_copy(
            g_hbm.at[pl.ds(2 * t, 2)], g_v.at[pl.ds(2 * t, 2)], g_sem.at[t]
        )
        for t in range(TILES)
    ]
    for copy in g_in:
        copy.start()

    def send_slot(dest):
        slot = jnp.int32(0)
        for b in range(NB):
            source = plan[dest * NB + b]
            slot = jnp.where((source >> 3) == me, source & 7, slot)
        return slot

    def back_slot(dest):
        slot = jnp.int32(0)
        for b in range(NB):
            slot = jnp.where((plan[me * NB + b] >> 3) == dest, b, slot)
        return slot

    def moved(stage, landing, kind, dest, h):
        return pltpu.make_async_remote_copy(
            src_ref=stage.at[dest, pl.ds(64 * h, 64)],
            dst_ref=landing.at[me, pl.ds(64 * h, 64)],
            send_sem=send_sem.at[kind],
            recv_sem=recv_sem.at[kind],
            device_id={"dp": dest},
            device_id_type=MESH,
        )

    def all_moved(stage, landing, kind):
        rest = pl.ds(0, RANKS - 1)
        return pltpu.make_async_remote_copy(
            src_ref=stage.at[rest],
            dst_ref=landing.at[rest],
            send_sem=send_sem.at[kind],
            recv_sem=recv_sem.at[kind],
            device_id={"dp": lax.rem(me + 1, RANKS)},
            device_id_type=MESH,
        )

    def round_of(stage, landing, kind, half, fill):
        def one(o, carry):
            dxs, dys = carry
            x = lax.rem(my_x + lax.rem(dxs, SIDE), SIDE)
            y = lax.rem(my_y + lax.rem(dys, SIDE), SIDE)
            dest = x * SIDE + y
            if half == 0:
                fill(stage, dest, dest)
            moved(stage, landing, kind, dest, half).start()
            return dxs // SIDE, dys // SIDE

        lax.fori_loop(1, RANKS, one, (DX + core * (DY - DX), DY + core * (DX - DY)))
        if half == 0:
            fill(landing, me, me)

    def exchange(fill, stage, landing, kind):
        for half in range(2):
            round_of(stage, landing, kind, half, fill)

    pl.when(core == 0)(k_in.wait)
    pl.when(core == 1)(v_in.wait)
    pl.semaphore_wait(barrier, RANKS - 1 + 4)

    def fill_kv(buffer, at, dest):
        buffer[at] = kv_v[send_slot(dest)]

    exchange(fill_kv, kv_s, kv_r, 5)

    q_in.wait()

    def fill_q(buffer, at, dest):
        buffer[at] = q_v[send_slot(dest)]

    exchange(fill_q, q_s, q_r, 0)

    w_in.wait()
    for t in range(TILES):
        g_in[t].wait()
    def project(t, carry):
        rows = pl.ds(2 * t, 2)
        product = dot(g_v[rows].reshape(TILE, D), w_v[...], NN)
        ga_v[rows] = product.astype(BF).reshape(2, RB, COLS)
        return carry

    lax.fori_loop(0, TILES, project, 0)

    def fill_ga(buffer, at, dest):
        buffer[at] = ga_v[send_slot(dest)]

    exchange(fill_ga, ga_s, ga_r, 1)

    factor = 0.1 * math.log(yarn_factor) + 1.0
    sign = jnp.where(lax.broadcasted_iota(jnp.int32, (1, RB), 1) < HD // 2, -factor, factor)
    for b in range(NB):
        mine = jnp.broadcast_to(seg[b : b + 1, :], (RB, RB)).T
        smaller = jnp.zeros((RB, RB), jnp.int32)
        for other in range(b + 1):
            smaller += jnp.where(seg[other : other + 1, :] < mine, 1, 0)
        first = jnp.sum(smaller, axis=1, keepdims=True)
        start[b] = jnp.broadcast_to(first, (RB, RB))

    def tables(b, carry):
        row = b * RB + lax.broadcasted_iota(jnp.int32, (RB, RB), 0)
        angle = (row - start[b]).astype(F32) * freq[0:1, :]
        cosf[b] = jnp.cos(angle) * factor
        sinf[b] = jnp.sin(angle) * sign
        return carry

    lax.fori_loop(0, NB, tables, 0)

    def find(g, carry):
        source = plan[g] - me * NB
        return tuple(jnp.where(source == j, g // NB, carry[j]) for j in range(NB))

    homes = lax.fori_loop(0, RANKS * NB, find, (jnp.int32(0),) * NB)

    def turned(x, cosine, sine):
        return x * cosine + pltpu.roll(x, HD // 2, 1) * sine

    def pair_copy(src, dst, i):
        return pltpu.make_async_remote_copy(
            src_ref=src, dst_ref=dst, send_sem=pair_send.at[i], recv_sem=pair_recv.at[i],
            device_id={"tensor": partner}, device_id_type=MESH,
        )

    all_moved(kv_s, kv_r, 5).wait_recv()
    is_key = (core == 0).astype(F32)

    def arrive_kv(b, carry):
        origin = plan[me * NB + b] >> 3
        x = kv_r[origin].astype(F32)
        cosine = cosf[b] * is_key + (1.0 - is_key)
        kv2[core, b] = turned(x, cosine, sinf[b] * is_key).astype(BF)
        return carry

    lax.fori_loop(0, NB, arrive_kv, 0)
    share_kv = pair_copy(kv2.at[core], kv2.at[core], 0)
    share_kv.start()

    all_moved(q_s, q_r, 0).wait_recv()
    for b in range(NB):
        block = q_r[plan[me * NB + b] >> 3]
        for h in range(2):
            x = block[:, h * HD : (h + 1) * HD].astype(F32)
            part = pl.ds((b % 2) * RB, RB)
            qs[b // 2 * 2 + h, part] = turned(x, cosf[b], sinf[b]).astype(BF)
    share_kv.wait_recv()

    def key_tile(kb):
        return kv2[0, 2 * kb : 2 * kb + 2].reshape(TILE, HD)

    def value_tile(kb):
        return kv2[1, 2 * kb : 2 * kb + 2].reshape(TILE, HD)

    column = lax.broadcasted_iota(jnp.int32, (TILE, TILE), 1)
    row_of = lax.broadcasted_iota(jnp.int32, (TILE, TILE), 0)
    for t in range(TILES):
        first = start[2 * t : 2 * t + 2].reshape(TILE, RB)
        first = jnp.concatenate([first, first], axis=1)

        def forward(h, carry):
            rows = qs[2 * t + h]
            scores = []
            for kb in range(t + 1):
                raw = dot(rows, key_tile(kb), NT)
                allowed = column + kb * TILE >= first
                if kb == t:
                    allowed = allowed & (column <= row_of)
                scores.append(jnp.where(allowed, raw, masked_score))
            peak = functools.reduce(jnp.maximum, scores)
            peak = jnp.max(peak, axis=1, keepdims=True)
            scores = [jnp.exp2((s - peak) * log2_scale) for s in scores]
            total = jnp.sum(functools.reduce(jnp.add, scores), axis=1, keepdims=True)
            share = 1.0 / total
            out = jnp.zeros((TILE, HD), F32)
            for kb in range(t + 1):
                p = scores[kb] * share
                prob[2 * t + h, :, kb * TILE : (kb + 1) * TILE] = p
                out += dot(p.astype(BF), value_tile(kb), NN)
            outs[2 * t : 2 * t + 2, h] = out.astype(BF).reshape(2, RB, HD)
            return carry

        lax.fori_loop(0, 2, forward, 0)

    def fill_out(buffer, at, dest):
        rows = outs[back_slot(dest)]
        for h in range(2):
            buffer[at, :, h * HD : (h + 1) * HD] = rows[h]

    exchange(fill_out, ao_s, ao_r, 2)

    all_moved(ga_s, ga_r, 1).wait_recv()
    for b in range(NB):
        block = ga_r[plan[me * NB + b] >> 3]
        for h in range(2):
            part = pl.ds((b % 2) * RB, RB)
            gas[b // 2 * 2 + h, part] = block[:, h * HD : (h + 1) * HD]

    dkt[...] = jnp.zeros_like(dkt)
    dvt[...] = jnp.zeros_like(dvt)
    for t in range(TILES):
        cosine = cosf[2 * t : 2 * t + 2].reshape(TILE, HD)
        sine = sinf[2 * t : 2 * t + 2].reshape(TILE, HD)

        def backward(h, carry):
            u = 2 * t + h
            upstream = gas[u]
            rows = qs[u]
            out = outs[2 * t : 2 * t + 2, h].reshape(TILE, HD)
            delta = jnp.sum(
                upstream.astype(F32) * out.astype(F32), axis=1, keepdims=True
            )
            dq = jnp.zeros((TILE, HD), F32)
            for kb in range(t + 1):
                cols = slice(kb * TILE, (kb + 1) * TILE)
                p = prob[u, :, cols]
                dp = dot(upstream, value_tile(kb), NT)
                ds = (p * (dp - delta)).astype(BF)
                dq += dot(ds, key_tile(kb), NN)
                dkt[:, cols] += dot(rows, ds, TN)
                dvt[:, cols] += dot(upstream, p.astype(BF), TN)
            dq = turned(dq * inv_scale, cosine, -sine).astype(BF)
            dq_v[2 * t : 2 * t + 2, h] = dq.reshape(2, RB, HD)
            return carry

        lax.fori_loop(0, 2, backward, 0)

    for b in range(NB):
        cols = slice(b * RB, (b + 1) * RB)
        dk = dkt[:, cols].T * inv_scale
        dkv_own[0, b] = turned(dk, cosf[b], -sinf[b]).astype(BF)
        dkv_own[1, b] = dvt[:, cols].T.astype(BF)
    share_dkv = pair_copy(dkv_own.at[1 - core], dkv_in, 1)
    share_dkv.start()

    def fill_dq(buffer, at, dest):
        rows = dq_v[back_slot(dest)]
        for h in range(2):
            buffer[at, :, h * HD : (h + 1) * HD] = rows[h]

    def fill_dkv(buffer, at, dest):
        buffer[at] = dkv_v[back_slot(dest)]

    share_dkv.wait_recv()
    for b in range(NB):
        dkv_v[b] = (dkv_own[core, b].astype(F32) + dkv_in[b].astype(F32)).astype(BF)
    exchange(fill_dkv, dkv_s, dkv_r, 3)

    all_moved(ao_s, ao_r, 2).wait_recv()
    for j in range(NB):
        aoh[j * RB : (j + 1) * RB] = ao_r[homes[j]]
    chunk = SIDE * WROWS
    for c in range(SIDE):
        rows = g_v[:, :, c * chunk : (c + 1) * chunk].reshape(NB * RB, chunk)
        term = dot(aoh[...], rows, TN).T.astype(BF)
        for e in range(SIDE):
            part = term[e * WROWS : (e + 1) * WROWS]
            w_s[0, c, e] = part[:, :HD]
            w_s[1, e, c] = part[:, HD:]

    mine = (my_x, my_y)

    def beside(axis, by):
        to = lax.rem(mine[axis] + by, SIDE)
        return to, (to * SIDE + my_y if axis == 0 else my_x * SIDE + to)

    def near(kind, half, way):
        to, dest = beside(half, (1, SIDE - 1)[way])
        relayed, plain = pl.ds(2 * way, 2), pl.ds(2 - 2 * way, 2)
        src, dst = (
            (w_s.at[half, lax.rem(mine[half] + 2, SIDE), relayed], w_r.at[half, way]),
            (w_s.at[half, to, plain], wn_r.at[half, way, plain]),
            (wb_s.at[half, way], wn_r.at[half, way, relayed]),
        )[kind]
        return pltpu.make_async_remote_copy(
            src_ref=src, dst_ref=dst,
            send_sem=w_send.at[kind, half, way], recv_sem=w_recv.at[kind, half, way],
            device_id={"dp": dest}, device_id_type=MESH,
        )

    def last(half, o):
        to, dest = beside(1 - half, o)
        return pltpu.make_async_remote_copy(
            src_ref=w2_s.at[half, to], dst_ref=w2_r.at[half, mine[1 - half]],
            send_sem=w2_send.at[half, o - 1], recv_sem=w2_recv.at[half, o - 1],
            device_id={"dp": dest}, device_id_type=MESH,
        )

    ways = [(half, way) for way in range(2) for half in range(2)]
    near_copies = [[near(kind, half, way) for half, way in ways] for kind in range(3)]
    last_copies = [last(half, o) for o in (1, 3, 2) for half in range(2)]
    for kind in range(2):
        for copy in near_copies[kind]:
            copy.start()
    for i, (half, way) in enumerate(ways):
        to, dest = beside(half, (1, SIDE - 1)[way])
        near_copies[0][i].wait_recv()
        both = w_r[half, way].astype(F32) + w_s[half, to, 2 * way : 2 * way + 2].astype(F32)
        wb_s[half, way] = both.astype(BF)
        near_copies[2][i].start()
    round_of(dq_s, dq_r, 4, 0, fill_dq)

    all_moved(dkv_s, dkv_r, 3).wait_recv()
    for j in range(NB):
        zk[core, zed, j] = dkv_r[homes[j]]
    z_copies = []
    for o in range(1, 4):
        copy = pltpu.make_async_remote_copy(
            src_ref=zk.at[core, zed], dst_ref=zk.at[core, zed],
            send_sem=z_send.at[o - 1], recv_sem=z_recv.at[o - 1],
            device_id={"tensor": lax.rem(zed + o, 4) * 2 + core}, device_id_type=MESH,
        )
        copy.start()
        z_copies.append(copy)

    for copy in near_copies[1] + near_copies[2]:
        copy.wait_recv()
    for half in range(2):
        for e in range(SIDE):
            total = w_s[half, mine[half], e].astype(F32)
            for way in range(2):
                total += wn_r[half, way, e].astype(F32)
            w2_s[half, e] = total.astype(BF)
    for copy in last_copies:
        copy.start()
    for half in range(2):
        w2_r[half, mine[1 - half]] = w2_s[half, mine[1 - half]]
    round_of(dq_s, dq_r, 4, 1, fill_dq)

    for copy in z_copies:
        copy.wait_recv()
    share_z = pair_copy(zk.at[core], zk.at[core], 2)
    share_z.start()
    share_z.wait_recv()
    copies = []
    for k, target in enumerate((gk_hbm, gv_hbm)):
        for z in range(KV):
            copy = pltpu.make_async_copy(
                zk.at[k, z], target.at[:, :, z * HD : (z + 1) * HD], out_sem.at[1 + 4 * k + z]
            )
            copy.start()
            copies.append(copy)

    for copy in last_copies:
        copy.wait_recv()
    for half in range(2):
        total = jnp.zeros((WROWS, HD), F32)
        for r in range(SIDE):
            total += w2_r[half, r].astype(F32)
        gw_v[:, half * HD : (half + 1) * HD] = total * (1.0 / RANKS)
    gw_out = pltpu.make_async_copy(gw_v, gw_hbm, out_sem.at[9])
    gw_out.start()

    all_moved(dq_s, dq_r, 4).wait_recv()
    for j in range(NB):
        q_v[j] = dq_r[homes[j]]
    gq_out = pltpu.make_async_copy(q_v, gq_hbm, out_sem.at[0])
    gq_out.start()

    for kind, (stage, landing) in enumerate(
        ((q_s, q_r), (ga_s, ga_r), (ao_s, ao_r), (dkv_s, dkv_r), (dq_s, dq_r), (kv_s, kv_r))
    ):
        all_moved(stage, landing, kind).wait_send()
    for copy in near_copies[0] + near_copies[1] + near_copies[2] + last_copies:
        copy.wait_send()
    share_kv.wait_send()
    share_dkv.wait_send()
    share_z.wait_send()
    for copy in z_copies:
        copy.wait_send()
    gq_out.wait()
    for copy in copies:
        copy.wait()
    gw_out.wait()


def hand_on(*refs):
    source, target, held, sems = refs[:4], refs[4:8], refs[8:12], refs[12]
    parts = []
    for k in range(4):
        half = source[k].shape[0] // 2
        for h in range(2):
            part = pl.ds(h * half, half)
            sem = sems.at[2 * k + h]
            parts.append(
                (
                    pltpu.make_async_copy(source[k].at[part], held[k].at[part], sem),
                    pltpu.make_async_copy(held[k].at[part], target[k].at[part], sem),
                )
            )
    for load, store in parts:
        load.start()
    for load, store in parts:
        load.wait()
        store.start()
    for load, store in parts:
        store.wait()


def local(query, key, value, grad_out, out_weight, plan, segments):
    blocked = (NB, RB)
    half = yarn_frequencies(HD)
    freq = np.tile(np.concatenate([half, half]), (8, 1)).astype(np.float32)
    hbm = pl.BlockSpec(memory_space=pl.ANY)
    vmem = pl.BlockSpec(memory_space=pltpu.VMEM)
    V = pltpu.VMEM
    dma = pltpu.SemaphoreType.DMA
    rows = NB * RB
    gq, gk, gv, gw = pl.pallas_call(
        kernel,
        out_shape=(
            jax.ShapeDtypeStruct(blocked + (COLS,), BF),
            jax.ShapeDtypeStruct(blocked + (KV * HD,), BF),
            jax.ShapeDtypeStruct(blocked + (KV * HD,), BF),
            jax.ShapeDtypeStruct((WROWS, COLS), F32),
        ),
        in_specs=[pl.BlockSpec(memory_space=pltpu.SMEM), vmem, vmem] + [hbm] * 5,
        out_specs=(hbm,) * 4,
        scratch_shapes=[
            V(blocked + (COLS,), BF),
            V(blocked + (HD,), BF),
            V(blocked + (D,), BF),
            V((D, COLS), BF),
            V((RANKS, RB, COLS), BF),
            V((RANKS, RB, COLS), BF),
            V((RANKS, RB, HD), BF),
            V((RANKS, RB, HD), BF),
            V(blocked + (COLS,), BF),
            V((RANKS, RB, COLS), BF),
            V((RANKS, RB, COLS), BF),
            V((2,) + blocked + (HD,), BF),
            V((2 * TILES, TILE, HD), BF),
            V((2 * TILES, TILE, HD), BF),
            V((NB, 2, RB, HD), BF),
            V((2 * TILES, TILE, rows), F32),
            V((RANKS, RB, COLS), BF),
            V((RANKS, RB, COLS), BF),
            V((NB, 2, RB, HD), BF),
            V((RANKS, RB, COLS), BF),
            V((RANKS, RB, COLS), BF),
            V((HD, rows), F32),
            V((HD, rows), F32),
            V((2,) + blocked + (HD,), BF),
            V(blocked + (HD,), BF),
            V(blocked + (HD,), BF),
            V((RANKS, RB, HD), BF),
            V((RANKS, RB, HD), BF),
            V((2, SIDE, SIDE, WROWS, HD), BF),
            V((2, 2, 2, WROWS, HD), BF),
            V((2, 2, SIDE, WROWS, HD), BF),
            V((2, 2, 2, WROWS, HD), BF),
            V((2, SIDE, WROWS, HD), BF),
            V((2, SIDE, WROWS, HD), BF),
            V((2, KV) + blocked + (HD,), BF),
            V((rows, COLS), BF),
            V((WROWS, COLS), F32),
            V(blocked + (HD,), F32),
            V(blocked + (HD,), F32),
            V(blocked + (RB,), jnp.int32),
            dma((3,)),
            dma((TILES,)),
            dma((6,)),
            dma((6,)),
            dma((3,)),
            dma((3,)),
            dma((3,)),
            dma((3,)),
            dma((3, 2, 2)),
            dma((3, 2, 2)),
            dma((2, 3)),
            dma((2, 3)),
            dma((10,)),
        ],
        compiler_params=pltpu.CompilerParams(
            collective_id=0, has_side_effects=True, vmem_limit_bytes=60 * 2**20
        ),
        cost_estimate=pl.CostEstimate(
            flops=7 * 10**9, bytes_accessed=14 * 2**20, transcendentals=2 * 10**6
        ),
    )(
        plan,
        segments.reshape(NB, RB),
        freq,
        query.reshape(blocked + (COLS,)),
        key.reshape(blocked + (KV * HD,)),
        value.reshape(blocked + (KV * HD,)),
        grad_out.reshape(blocked + (D,)),
        out_weight,
    )
    gq, gk, gv, gw = pl.pallas_call(
        hand_on,
        out_shape=tuple(jax.ShapeDtypeStruct(x.shape, x.dtype) for x in (gq, gk, gv, gw)),
        in_specs=[hbm] * 4,
        out_specs=(hbm,) * 4,
        scratch_shapes=[V(x.shape, x.dtype) for x in (gq, gk, gv, gw)] + [dma((8,))],
    )(gq, gk, gv, gw)
    return (
        gq.reshape(rows, COLS),
        gk.reshape(rows, KV * HD),
        gv.reshape(rows, KV * HD),
        gw,
    )


def solution(mesh):
    in_specs = (
        P("dp", "tensor"),
        P("dp", None),
        P("dp", None),
        P("dp", None),
        P(None, "tensor"),
        P(),
        P("dp"),
    )
    out_specs = (P("dp", "tensor"), P("dp", None), P("dp", None), P("dp", "tensor"))
    return jax.shard_map(local, mesh=mesh, in_specs=in_specs, out_specs=out_specs, check_vma=False)
```

```python
import functools
import math

import jax
import jax.numpy as jnp
import numpy as np
from jax import lax
from jax.experimental import pallas as pl
from jax.experimental.pallas import tpu as pltpu
from jax.sharding import PartitionSpec as P

D = 3584
KV = 4
HD = 128
HEADS = 16
RB = 128
NB = 8
RANKS = 16
LANES = 8
COLS = 256
TILE = 256
TILES = NB * RB // TILE
WROWS = D // RANKS
SIDE = 4
ORDER = (
    (2, 2), (1, 0), (0, 1), (1, 2), (3, 0), (0, 3), (2, 1), (1, 1),
    (3, 2), (2, 0), (3, 3), (2, 3), (0, 2), (1, 3), (3, 1),
)
DX = sum(dx << (2 * i) for i, (dx, dy) in enumerate(ORDER))
DY = sum(dy << (2 * i) for i, (dx, dy) in enumerate(ORDER))

rope_base = 1000000.0
yarn_factor = 4.0
yarn_context = 32768.0
beta_fast = 32.0
beta_slow = 1.0
masked_score = -1e30
MESH = pl.DeviceIdType.MESH
BF = jnp.bfloat16
F32 = jnp.float32


def yarn_frequencies(head_size):
    half_size = head_size // 2

    def correction(rotations):
        return (
            head_size
            * math.log(yarn_context / (rotations * 2.0 * math.pi))
            / (2.0 * math.log(rope_base))
        )

    lower_bound = max(math.floor(correction(beta_fast)), 0)
    upper_bound = min(math.ceil(correction(beta_slow)), head_size - 1)
    ramp_span = max(upper_bound - lower_bound, 0.001)
    row_index = np.arange(half_size).astype(np.float64)
    extrap_freq = rope_base ** (-2.0 * row_index / head_size)
    interp_freq = extrap_freq / yarn_factor
    ramp_weight = np.clip((row_index - lower_bound) / ramp_span, 0.0, 1.0)
    return interp_freq * ramp_weight + extrap_freq * (1.0 - ramp_weight)


def dot(a, b, dims):
    return lax.dot_general(a, b, (dims, ((), ())), preferred_element_type=F32)


NN = ((1,), (0,))
NT = ((1,), (1,))
TN = ((0,), (0,))


def kernel(
    plan, seg, freq, q_hbm, k_hbm, v_hbm, g_hbm, w_hbm,
    gq_hbm, gk_hbm, gv_hbm, gw_hbm,
    q_v, kv_v, g_v, w_v, q_s, q_r, kv_s, kv_r, ga_v, ga_s, ga_r, kv2, qs, gas, outs, prob,
    ao_s, ao_r, dq_v, dq_s, dq_r, dkt, dvt, dkv_own, dkv_in, dkv_v, dkv_s, dkv_r,
    w_s, w_r, wn_r, wb_s, w2_s, w2_r, zk, aoh, gw_v, cosf, sinf, start,
    in_sem, g_sem, send_sem, recv_sem, pair_send, pair_recv, z_send, z_recv, w_send, w_recv, w2_send, w2_recv, out_sem,
):
    me = lax.axis_index("dp")
    lane = lax.axis_index("tensor")
    core = lax.rem(lane, 2)
    zed = lane // 2
    partner = lane + 1 - 2 * core
    my_x = me // SIDE
    my_y = lax.rem(me, SIDE)
    inv_scale = 1.0 / math.sqrt(HD)
    log2_scale = inv_scale * math.log2(math.e)

    barrier = pltpu.get_barrier_semaphore()

    def greet(o, carry):
        pl.semaphore_signal(
            barrier, inc=1, device_id={"dp": lax.rem(me + o, RANKS)}, device_id_type=MESH
        )
        return carry

    lax.fori_loop(1, RANKS, greet, 0)
    pl.semaphore_signal(barrier, inc=1, device_id={"tensor": partner}, device_id_type=MESH)
    for o in range(1, 4):
        peer = lax.rem(zed + o, 4) * 2 + core
        pl.semaphore_signal(barrier, inc=1, device_id={"tensor": peer}, device_id_type=MESH)

    q_in = pltpu.make_async_copy(q_hbm, q_v, in_sem.at[0])
    q_in.start()
    head_cols = pl.ds(pl.multiple_of(zed * HD, HD), HD)
    k_in = pltpu.make_async_copy(k_hbm.at[:, :, head_cols], kv_v, in_sem.at[1])
    v_in = pltpu.make_async_copy(v_hbm.at[:, :, head_cols], kv_v, in_sem.at[1])
    pl.when(core == 0)(k_in.start)
    pl.when(core == 1)(v_in.start)
    w_in = pltpu.make_async_copy(w_hbm, w_v, in_sem.at[2])
    w_in.start()
    g_in = [
        pltpu.make_async_copy(
            g_hbm.at[pl.ds(2 * t, 2)], g_v.at[pl.ds(2 * t, 2)], g_sem.at[t]
        )
        for t in range(TILES)
    ]
    for copy in g_in:
        copy.start()

    def send_slot(dest):
        slot = jnp.int32(0)
        for b in range(NB):
            source = plan[dest * NB + b]
            slot = jnp.where((source >> 3) == me, source & 7, slot)
        return slot

    def back_slot(dest):
        slot = jnp.int32(0)
        for b in range(NB):
            slot = jnp.where((plan[me * NB + b] >> 3) == dest, b, slot)
        return slot

    def moved(stage, landing, kind, dest, h):
        return pltpu.make_async_remote_copy(
            src_ref=stage.at[dest, pl.ds(64 * h, 64)],
            dst_ref=landing.at[me, pl.ds(64 * h, 64)],
            send_sem=send_sem.at[kind],
            recv_sem=recv_sem.at[kind],
            device_id={"dp": dest},
            device_id_type=MESH,
        )

    def all_moved(stage, landing, kind):
        rest = pl.ds(0, RANKS - 1)
        return pltpu.make_async_remote_copy(
            src_ref=stage.at[rest],
            dst_ref=landing.at[rest],
            send_sem=send_sem.at[kind],
            recv_sem=recv_sem.at[kind],
            device_id={"dp": lax.rem(me + 1, RANKS)},
            device_id_type=MESH,
        )

    def round_of(stage, landing, kind, half, fill):
        def one(o, carry):
            dxs, dys = carry
            x = lax.rem(my_x + lax.rem(dxs, SIDE), SIDE)
            y = lax.rem(my_y + lax.rem(dys, SIDE), SIDE)
            dest = x * SIDE + y
            if half == 0:
                fill(stage, dest, dest)
            moved(stage, landing, kind, dest, half).start()
            return dxs // SIDE, dys // SIDE

        lax.fori_loop(1, RANKS, one, (DX + core * (DY - DX), DY + core * (DX - DY)))
        if half == 0:
            fill(landing, me, me)

    def exchange(fill, stage, landing, kind):
        for half in range(2):
            round_of(stage, landing, kind, half, fill)

    pl.when(core == 0)(k_in.wait)
    pl.when(core == 1)(v_in.wait)
    pl.semaphore_wait(barrier, RANKS - 1 + 4)

    def fill_kv(buffer, at, dest):
        buffer[at] = kv_v[send_slot(dest)]

    exchange(fill_kv, kv_s, kv_r, 5)

    q_in.wait()

    def fill_q(buffer, at, dest):
        buffer[at] = q_v[send_slot(dest)]

    exchange(fill_q, q_s, q_r, 0)

    w_in.wait()
    for t in range(TILES):
        g_in[t].wait()
    def project(t, carry):
        rows = pl.ds(2 * t, 2)
        product = dot(g_v[rows].reshape(TILE, D), w_v[...], NN)
        ga_v[rows] = product.astype(BF).reshape(2, RB, COLS)
        return carry

    lax.fori_loop(0, TILES, project, 0)

    def fill_ga(buffer, at, dest):
        buffer[at] = ga_v[send_slot(dest)]

    exchange(fill_ga, ga_s, ga_r, 1)

    factor = 0.1 * math.log(yarn_factor) + 1.0
    sign = jnp.where(lax.broadcasted_iota(jnp.int32, (1, RB), 1) < HD // 2, -factor, factor)
    for b in range(NB):
        mine = jnp.broadcast_to(seg[b : b + 1, :], (RB, RB)).T
        smaller = jnp.zeros((RB, RB), jnp.int32)
        for other in range(b + 1):
            smaller += jnp.where(seg[other : other + 1, :] < mine, 1, 0)
        first = jnp.sum(smaller, axis=1, keepdims=True)
        start[b] = jnp.broadcast_to(first, (RB, RB))

    def tables(b, carry):
        row = b * RB + lax.broadcasted_iota(jnp.int32, (RB, RB), 0)
        angle = (row - start[b]).astype(F32) * freq[0:1, :]
        cosf[b] = jnp.cos(angle) * factor
        sinf[b] = jnp.sin(angle) * sign
        return carry

    lax.fori_loop(0, NB, tables, 0)

    def find(g, carry):
        source = plan[g] - me * NB
        return tuple(jnp.where(source == j, g // NB, carry[j]) for j in range(NB))

    homes = lax.fori_loop(0, RANKS * NB, find, (jnp.int32(0),) * NB)

    def turned(x, cosine, sine):
        return x * cosine + pltpu.roll(x, HD // 2, 1) * sine

    def pair_copy(src, dst, i):
        return pltpu.make_async_remote_copy(
            src_ref=src, dst_ref=dst, send_sem=pair_send.at[i], recv_sem=pair_recv.at[i],
            device_id={"tensor": partner}, device_id_type=MESH,
        )

    all_moved(kv_s, kv_r, 5).wait_recv()
    is_key = (core == 0).astype(F32)

    def arrive_kv(b, carry):
        origin = plan[me * NB + b] >> 3
        x = kv_r[origin].astype(F32)
        cosine = cosf[b] * is_key + (1.0 - is_key)
        kv2[core, b] = turned(x, cosine, sinf[b] * is_key).astype(BF)
        return carry

    lax.fori_loop(0, NB, arrive_kv, 0)
    share_kv = pair_copy(kv2.at[core], kv2.at[core], 0)
    share_kv.start()

    all_moved(q_s, q_r, 0).wait_recv()
    for b in range(NB):
        block = q_r[plan[me * NB + b] >> 3]
        for h in range(2):
            x = block[:, h * HD : (h + 1) * HD].astype(F32)
            part = pl.ds((b % 2) * RB, RB)
            qs[b // 2 * 2 + h, part] = turned(x, cosf[b], sinf[b]).astype(BF)
    share_kv.wait_recv()

    def key_tile(kb):
        return kv2[0, 2 * kb : 2 * kb + 2].reshape(TILE, HD)

    def value_tile(kb):
        return kv2[1, 2 * kb : 2 * kb + 2].reshape(TILE, HD)

    column = lax.broadcasted_iota(jnp.int32, (TILE, TILE), 1)
    row_of = lax.broadcasted_iota(jnp.int32, (TILE, TILE), 0)
    for t in range(TILES):
        first = start[2 * t : 2 * t + 2].reshape(TILE, RB)
        first = jnp.concatenate([first, first], axis=1)

        def forward(h, carry):
            rows = qs[2 * t + h]
            scores = []
            for kb in range(t + 1):
                raw = dot(rows, key_tile(kb), NT)
                allowed = column + kb * TILE >= first
                if kb == t:
                    allowed = allowed & (column <= row_of)
                scores.append(jnp.where(allowed, raw, masked_score))
            peak = functools.reduce(jnp.maximum, scores)
            peak = jnp.max(peak, axis=1, keepdims=True)
            scores = [jnp.exp2((s - peak) * log2_scale) for s in scores]
            total = jnp.sum(functools.reduce(jnp.add, scores), axis=1, keepdims=True)
            share = 1.0 / total
            out = jnp.zeros((TILE, HD), F32)
            for kb in range(t + 1):
                p = scores[kb] * share
                prob[2 * t + h, :, kb * TILE : (kb + 1) * TILE] = p
                out += dot(p.astype(BF), value_tile(kb), NN)
            outs[2 * t : 2 * t + 2, h] = out.astype(BF).reshape(2, RB, HD)
            return carry

        lax.fori_loop(0, 2, forward, 0)

    def fill_out(buffer, at, dest):
        rows = outs[back_slot(dest)]
        for h in range(2):
            buffer[at, :, h * HD : (h + 1) * HD] = rows[h]

    exchange(fill_out, ao_s, ao_r, 2)

    all_moved(ga_s, ga_r, 1).wait_recv()
    for b in range(NB):
        block = ga_r[plan[me * NB + b] >> 3]
        for h in range(2):
            part = pl.ds((b % 2) * RB, RB)
            gas[b // 2 * 2 + h, part] = block[:, h * HD : (h + 1) * HD]

    dkt[...] = jnp.zeros_like(dkt)
    dvt[...] = jnp.zeros_like(dvt)
    for t in range(TILES):
        cosine = cosf[2 * t : 2 * t + 2].reshape(TILE, HD)
        sine = sinf[2 * t : 2 * t + 2].reshape(TILE, HD)

        def backward(h, carry):
            u = 2 * t + h
            upstream = gas[u]
            rows = qs[u]
            out = outs[2 * t : 2 * t + 2, h].reshape(TILE, HD)
            delta = jnp.sum(
                upstream.astype(F32) * out.astype(F32), axis=1, keepdims=True
            )
            dq = jnp.zeros((TILE, HD), F32)
            for kb in range(t + 1):
                cols = slice(kb * TILE, (kb + 1) * TILE)
                p = prob[u, :, cols]
                dp = dot(upstream, value_tile(kb), NT)
                ds = (p * (dp - delta)).astype(BF)
                dq += dot(ds, key_tile(kb), NN)
                dkt[:, cols] += dot(rows, ds, TN)
                dvt[:, cols] += dot(upstream, p.astype(BF), TN)
            dq = turned(dq * inv_scale, cosine, -sine).astype(BF)
            dq_v[2 * t : 2 * t + 2, h] = dq.reshape(2, RB, HD)
            return carry

        lax.fori_loop(0, 2, backward, 0)

    for b in range(NB):
        cols = slice(b * RB, (b + 1) * RB)
        dk = dkt[:, cols].T * inv_scale
        dkv_own[0, b] = turned(dk, cosf[b], -sinf[b]).astype(BF)
        dkv_own[1, b] = dvt[:, cols].T.astype(BF)
    share_dkv = pair_copy(dkv_own.at[1 - core], dkv_in, 1)
    share_dkv.start()

    def fill_dq(buffer, at, dest):
        rows = dq_v[back_slot(dest)]
        for h in range(2):
            buffer[at, :, h * HD : (h + 1) * HD] = rows[h]

    def fill_dkv(buffer, at, dest):
        buffer[at] = dkv_v[back_slot(dest)]

    share_dkv.wait_recv()
    for b in range(NB):
        dkv_v[b] = (dkv_own[core, b].astype(F32) + dkv_in[b].astype(F32)).astype(BF)
    exchange(fill_dkv, dkv_s, dkv_r, 3)

    all_moved(ao_s, ao_r, 2).wait_recv()
    for j in range(NB):
        aoh[j * RB : (j + 1) * RB] = ao_r[homes[j]]
    chunk = SIDE * WROWS
    for c in range(SIDE):
        rows = g_v[:, :, c * chunk : (c + 1) * chunk].reshape(NB * RB, chunk)
        term = dot(aoh[...], rows, TN).T.astype(BF)
        for e in range(SIDE):
            part = term[e * WROWS : (e + 1) * WROWS]
            w_s[0, c, e] = part[:, :HD]
            w_s[1, e, c] = part[:, HD:]

    mine = (my_x, my_y)

    def beside(axis, by):
        to = lax.rem(mine[axis] + by, SIDE)
        return to, (to * SIDE + my_y if axis == 0 else my_x * SIDE + to)

    def near(kind, half, way):
        to, dest = beside(half, (1, SIDE - 1)[way])
        relayed, plain = pl.ds(2 * way, 2), pl.ds(2 - 2 * way, 2)
        src, dst = (
            (w_s.at[half, lax.rem(mine[half] + 2, SIDE), relayed], w_r.at[half, way]),
            (w_s.at[half, to, plain], wn_r.at[half, way, plain]),
            (wb_s.at[half, way], wn_r.at[half, way, relayed]),
        )[kind]
        return pltpu.make_async_remote_copy(
            src_ref=src, dst_ref=dst,
            send_sem=w_send.at[kind, half, way], recv_sem=w_recv.at[kind, half, way],
            device_id={"dp": dest}, device_id_type=MESH,
        )

    def last(half, o):
        to, dest = beside(1 - half, o)
        return pltpu.make_async_remote_copy(
            src_ref=w2_s.at[half, to], dst_ref=w2_r.at[half, mine[1 - half]],
            send_sem=w2_send.at[half, o - 1], recv_sem=w2_recv.at[half, o - 1],
            device_id={"dp": dest}, device_id_type=MESH,
        )

    ways = [(half, way) for way in range(2) for half in range(2)]
    near_copies = [[near(kind, half, way) for half, way in ways] for kind in range(3)]
    last_copies = [last(half, o) for o in (1, 3, 2) for half in range(2)]
    for copy in near_copies[0]:
        copy.start()
    for copy in near_copies[1]:
        copy.start()
    all_moved(dkv_s, dkv_r, 3).wait_recv()
    for j in range(NB):
        zk[core, zed, j] = dkv_r[homes[j]]
    z_copies = []
    for o in range(1, 4):
        copy = pltpu.make_async_remote_copy(
            src_ref=zk.at[core, zed], dst_ref=zk.at[core, zed],
            send_sem=z_send.at[o - 1], recv_sem=z_recv.at[o - 1],
            device_id={"tensor": lax.rem(zed + o, 4) * 2 + core}, device_id_type=MESH,
        )
        copy.start()
        z_copies.append(copy)

    for i, (half, way) in enumerate(ways):
        to, dest = beside(half, (1, SIDE - 1)[way])
        near_copies[0][i].wait_recv()
        both = w_r[half, way].astype(F32) + w_s[half, to, 2 * way : 2 * way + 2].astype(F32)
        wb_s[half, way] = both.astype(BF)
        near_copies[2][i].start()
    round_of(dq_s, dq_r, 4, 0, fill_dq)

    for copy in near_copies[1] + near_copies[2]:
        copy.wait_recv()
    for half in range(2):
        for e in range(SIDE):
            total = w_s[half, mine[half], e].astype(F32)
            for way in range(2):
                total += wn_r[half, way, e].astype(F32)
            w2_s[half, e] = total.astype(BF)
    for copy in last_copies:
        copy.start()
    for half in range(2):
        w2_r[half, mine[1 - half]] = w2_s[half, mine[1 - half]]
    round_of(dq_s, dq_r, 4, 1, fill_dq)

    for copy in z_copies:
        copy.wait_recv()
    share_z = pair_copy(zk.at[core], zk.at[core], 2)
    share_z.start()
    share_z.wait_recv()
    copies = []
    for k, target in enumerate((gk_hbm, gv_hbm)):
        for z in range(KV):
            copy = pltpu.make_async_copy(
                zk.at[k, z], target.at[:, :, z * HD : (z + 1) * HD], out_sem.at[1 + 4 * k + z]
            )
            copy.start()
            copies.append(copy)

    for copy in last_copies:
        copy.wait_recv()
    for half in range(2):
        total = jnp.zeros((WROWS, HD), F32)
        for r in range(SIDE):
            total += w2_r[half, r].astype(F32)
        gw_v[:, half * HD : (half + 1) * HD] = total * (1.0 / RANKS)
    gw_out = pltpu.make_async_copy(gw_v, gw_hbm, out_sem.at[9])
    gw_out.start()

    all_moved(dq_s, dq_r, 4).wait_recv()
    for j in range(NB):
        q_v[j] = dq_r[homes[j]]
    gq_out = pltpu.make_async_copy(q_v, gq_hbm, out_sem.at[0])
    gq_out.start()

    for kind, (stage, landing) in enumerate(
        ((q_s, q_r), (ga_s, ga_r), (ao_s, ao_r), (dkv_s, dkv_r), (dq_s, dq_r), (kv_s, kv_r))
    ):
        all_moved(stage, landing, kind).wait_send()
    for copy in near_copies[0] + near_copies[1] + near_copies[2] + last_copies:
        copy.wait_send()
    share_kv.wait_send()
    share_dkv.wait_send()
    share_z.wait_send()
    for copy in z_copies:
        copy.wait_send()
    gq_out.wait()
    for copy in copies:
        copy.wait()
    gw_out.wait()


def hand_on(*refs):
    source, target, held, sems = refs[:4], refs[4:8], refs[8:12], refs[12]
    parts = []
    for k in range(4):
        half = source[k].shape[0] // 2
        for h in range(2):
            part = pl.ds(h * half, half)
            sem = sems.at[2 * k + h]
            parts.append(
                (
                    pltpu.make_async_copy(source[k].at[part], held[k].at[part], sem),
                    pltpu.make_async_copy(held[k].at[part], target[k].at[part], sem),
                )
            )
    for load, store in parts:
        load.start()
    for load, store in parts:
        load.wait()
        store.start()
    for load, store in parts:
        store.wait()


def local(query, key, value, grad_out, out_weight, plan, segments):
    blocked = (NB, RB)
    half = yarn_frequencies(HD)
    freq = np.tile(np.concatenate([half, half]), (8, 1)).astype(np.float32)
    hbm = pl.BlockSpec(memory_space=pl.ANY)
    vmem = pl.BlockSpec(memory_space=pltpu.VMEM)
    V = pltpu.VMEM
    dma = pltpu.SemaphoreType.DMA
    rows = NB * RB
    gq, gk, gv, gw = pl.pallas_call(
        kernel,
        out_shape=(
            jax.ShapeDtypeStruct(blocked + (COLS,), BF),
            jax.ShapeDtypeStruct(blocked + (KV * HD,), BF),
            jax.ShapeDtypeStruct(blocked + (KV * HD,), BF),
            jax.ShapeDtypeStruct((WROWS, COLS), F32),
        ),
        in_specs=[pl.BlockSpec(memory_space=pltpu.SMEM), vmem, vmem] + [hbm] * 5,
        out_specs=(hbm,) * 4,
        scratch_shapes=[
            V(blocked + (COLS,), BF),
            V(blocked + (HD,), BF),
            V(blocked + (D,), BF),
            V((D, COLS), BF),
            V((RANKS, RB, COLS), BF),
            V((RANKS, RB, COLS), BF),
            V((RANKS, RB, HD), BF),
            V((RANKS, RB, HD), BF),
            V(blocked + (COLS,), BF),
            V((RANKS, RB, COLS), BF),
            V((RANKS, RB, COLS), BF),
            V((2,) + blocked + (HD,), BF),
            V((2 * TILES, TILE, HD), BF),
            V((2 * TILES, TILE, HD), BF),
            V((NB, 2, RB, HD), BF),
            V((2 * TILES, TILE, rows), F32),
            V((RANKS, RB, COLS), BF),
            V((RANKS, RB, COLS), BF),
            V((NB, 2, RB, HD), BF),
            V((RANKS, RB, COLS), BF),
            V((RANKS, RB, COLS), BF),
            V((HD, rows), F32),
            V((HD, rows), F32),
            V((2,) + blocked + (HD,), BF),
            V(blocked + (HD,), BF),
            V(blocked + (HD,), BF),
            V((RANKS, RB, HD), BF),
            V((RANKS, RB, HD), BF),
            V((2, SIDE, SIDE, WROWS, HD), BF),
            V((2, 2, 2, WROWS, HD), BF),
            V((2, 2, SIDE, WROWS, HD), BF),
            V((2, 2, 2, WROWS, HD), BF),
            V((2, SIDE, WROWS, HD), BF),
            V((2, SIDE, WROWS, HD), BF),
            V((2, KV) + blocked + (HD,), BF),
            V((rows, COLS), BF),
            V((WROWS, COLS), F32),
            V(blocked + (HD,), F32),
            V(blocked + (HD,), F32),
            V(blocked + (RB,), jnp.int32),
            dma((3,)),
            dma((TILES,)),
            dma((6,)),
            dma((6,)),
            dma((3,)),
            dma((3,)),
            dma((3,)),
            dma((3,)),
            dma((3, 2, 2)),
            dma((3, 2, 2)),
            dma((2, 3)),
            dma((2, 3)),
            dma((10,)),
        ],
        compiler_params=pltpu.CompilerParams(
            collective_id=0, has_side_effects=True, vmem_limit_bytes=60 * 2**20
        ),
        cost_estimate=pl.CostEstimate(
            flops=7 * 10**9, bytes_accessed=14 * 2**20, transcendentals=2 * 10**6
        ),
    )(
        plan,
        segments.reshape(NB, RB),
        freq,
        query.reshape(blocked + (COLS,)),
        key.reshape(blocked + (KV * HD,)),
        value.reshape(blocked + (KV * HD,)),
        grad_out.reshape(blocked + (D,)),
        out_weight,
    )
    gq, gk, gv, gw = pl.pallas_call(
        hand_on,
        out_shape=tuple(jax.ShapeDtypeStruct(x.shape, x.dtype) for x in (gq, gk, gv, gw)),
        in_specs=[hbm] * 4,
        out_specs=(hbm,) * 4,
        scratch_shapes=[V(x.shape, x.dtype) for x in (gq, gk, gv, gw)] + [dma((8,))],
    )(gq, gk, gv, gw)
    return (
        gq.reshape(rows, COLS),
        gk.reshape(rows, KV * HD),
        gv.reshape(rows, KV * HD),
        gw,
    )


def solution(mesh):
    in_specs = (
        P("dp", "tensor"),
        P("dp", None),
        P("dp", None),
        P("dp", None),
        P(None, "tensor"),
        P(),
        P("dp"),
    )
    out_specs = (P("dp", "tensor"), P("dp", None), P("dp", None), P("dp", "tensor"))
    return jax.shard_map(local, mesh=mesh, in_specs=in_specs, out_specs=out_specs, check_vma=False)
```

```python
import functools
import math

import jax
import jax.numpy as jnp
import numpy as np
from jax import lax
from jax.experimental import pallas as pl
from jax.experimental.pallas import tpu as pltpu
from jax.sharding import PartitionSpec as P

D = 3584
KV = 4
HD = 128
HEADS = 16
RB = 128
NB = 8
RANKS = 16
LANES = 8
COLS = 256
TILE = 256
TILES = NB * RB // TILE
WROWS = D // RANKS
SIDE = 4
ORDER = (
    (2, 2), (1, 0), (0, 1), (1, 2), (3, 0), (0, 3), (2, 1), (1, 1),
    (3, 2), (2, 0), (3, 3), (2, 3), (0, 2), (1, 3), (3, 1),
)
DX = sum(dx << (2 * i) for i, (dx, dy) in enumerate(ORDER))
DY = sum(dy << (2 * i) for i, (dx, dy) in enumerate(ORDER))

rope_base = 1000000.0
yarn_factor = 4.0
yarn_context = 32768.0
beta_fast = 32.0
beta_slow = 1.0
masked_score = -1e30
MESH = pl.DeviceIdType.MESH
BF = jnp.bfloat16
F32 = jnp.float32


def yarn_frequencies(head_size):
    half_size = head_size // 2

    def correction(rotations):
        return (
            head_size
            * math.log(yarn_context / (rotations * 2.0 * math.pi))
            / (2.0 * math.log(rope_base))
        )

    lower_bound = max(math.floor(correction(beta_fast)), 0)
    upper_bound = min(math.ceil(correction(beta_slow)), head_size - 1)
    ramp_span = max(upper_bound - lower_bound, 0.001)
    row_index = np.arange(half_size).astype(np.float64)
    extrap_freq = rope_base ** (-2.0 * row_index / head_size)
    interp_freq = extrap_freq / yarn_factor
    ramp_weight = np.clip((row_index - lower_bound) / ramp_span, 0.0, 1.0)
    return interp_freq * ramp_weight + extrap_freq * (1.0 - ramp_weight)


def dot(a, b, dims):
    return lax.dot_general(a, b, (dims, ((), ())), preferred_element_type=F32)


NN = ((1,), (0,))
NT = ((1,), (1,))
TN = ((0,), (0,))


def kernel(
    plan, seg, freq, q_hbm, k_hbm, v_hbm, g_hbm, w_hbm,
    gq_hbm, gk_hbm, gv_hbm, gw_hbm,
    q_v, kv_v, g_v, w_v, q_s, q_r, kv_s, kv_r, ga_v, ga_s, ga_r, kv2, qs, gas, outs, prob,
    ao_s, ao_r, dq_v, dq_s, dq_r, dkt, dvt, dkv_own, dkv_in, dkv_v, dkv_s, dkv_r,
    w_s, w_r, wn_r, wb_s, w2_s, w2_r, zk, aoh, gw_v, cosf, sinf, start,
    in_sem, g_sem, send_sem, recv_sem, pair_send, pair_recv, z_send, z_recv, w_send, w_recv, w2_send, w2_recv, out_sem,
):
    me = lax.axis_index("dp")
    lane = lax.axis_index("tensor")
    core = lax.rem(lane, 2)
    zed = lane // 2
    partner = lane + 1 - 2 * core
    my_x = me // SIDE
    my_y = lax.rem(me, SIDE)
    inv_scale = 1.0 / math.sqrt(HD)
    log2_scale = inv_scale * math.log2(math.e)

    barrier = pltpu.get_barrier_semaphore()

    def greet(o, carry):
        pl.semaphore_signal(
            barrier, inc=1, device_id={"dp": lax.rem(me + o, RANKS)}, device_id_type=MESH
        )
        return carry

    lax.fori_loop(1, RANKS, greet, 0)
    pl.semaphore_signal(barrier, inc=1, device_id={"tensor": partner}, device_id_type=MESH)
    for o in range(1, 4):
        peer = lax.rem(zed + o, 4) * 2 + core
        pl.semaphore_signal(barrier, inc=1, device_id={"tensor": peer}, device_id_type=MESH)

    q_in = pltpu.make_async_copy(q_hbm, q_v, in_sem.at[0])
    q_in.start()
    head_cols = pl.ds(pl.multiple_of(zed * HD, HD), HD)
    k_in = pltpu.make_async_copy(k_hbm.at[:, :, head_cols], kv_v, in_sem.at[1])
    v_in = pltpu.make_async_copy(v_hbm.at[:, :, head_cols], kv_v, in_sem.at[1])
    pl.when(core == 0)(k_in.start)
    pl.when(core == 1)(v_in.start)
    w_in = pltpu.make_async_copy(w_hbm, w_v, in_sem.at[2])
    w_in.start()
    g_in = [
        pltpu.make_async_copy(
            g_hbm.at[pl.ds(2 * t, 2)], g_v.at[pl.ds(2 * t, 2)], g_sem.at[t]
        )
        for t in range(TILES)
    ]
    for copy in g_in:
        copy.start()

    def send_slot(dest):
        slot = jnp.int32(0)
        for b in range(NB):
            source = plan[dest * NB + b]
            slot = jnp.where((source >> 3) == me, source & 7, slot)
        return slot

    def back_slot(dest):
        slot = jnp.int32(0)
        for b in range(NB):
            slot = jnp.where((plan[me * NB + b] >> 3) == dest, b, slot)
        return slot

    def moved(stage, landing, kind, dest, first, count):
        return pltpu.make_async_remote_copy(
            src_ref=stage.at[dest, pl.ds(first, count)],
            dst_ref=landing.at[me, pl.ds(first, count)],
            send_sem=send_sem.at[kind],
            recv_sem=recv_sem.at[kind],
            device_id={"dp": dest},
            device_id_type=MESH,
        )

    def all_moved(stage, landing, kind):
        rest = pl.ds(0, RANKS - 1)
        return pltpu.make_async_remote_copy(
            src_ref=stage.at[rest],
            dst_ref=landing.at[rest],
            send_sem=send_sem.at[kind],
            recv_sem=recv_sem.at[kind],
            device_id={"dp": lax.rem(me + 1, RANKS)},
            device_id_type=MESH,
        )

    def round_of(stage, landing, kind, first, count, fill):
        def one(o, carry):
            dxs, dys = carry
            x = lax.rem(my_x + lax.rem(dxs, SIDE), SIDE)
            y = lax.rem(my_y + lax.rem(dys, SIDE), SIDE)
            dest = x * SIDE + y
            if first == 0:
                fill(stage, dest, dest)
            moved(stage, landing, kind, dest, first, count).start()
            return dxs // SIDE, dys // SIDE

        lax.fori_loop(1, RANKS, one, (DX + core * (DY - DX), DY + core * (DX - DY)))
        if first == 0:
            fill(landing, me, me)

    def exchange(fill, stage, landing, kind, rounds=2):
        count = RB // rounds
        for part in range(rounds):
            round_of(stage, landing, kind, part * count, count, fill)

    pl.when(core == 0)(k_in.wait)
    pl.when(core == 1)(v_in.wait)
    pl.semaphore_wait(barrier, RANKS - 1 + 4)

    def fill_kv(buffer, at, dest):
        buffer[at] = kv_v[send_slot(dest)]

    exchange(fill_kv, kv_s, kv_r, 5, 1)

    q_in.wait()

    def fill_q(buffer, at, dest):
        buffer[at] = q_v[send_slot(dest)]

    exchange(fill_q, q_s, q_r, 0)

    w_in.wait()
    for t in range(TILES):
        g_in[t].wait()
    def project(t, carry):
        rows = pl.ds(2 * t, 2)
        product = dot(g_v[rows].reshape(TILE, D), w_v[...], NN)
        ga_v[rows] = product.astype(BF).reshape(2, RB, COLS)
        return carry

    lax.fori_loop(0, TILES, project, 0)

    def fill_ga(buffer, at, dest):
        buffer[at] = ga_v[send_slot(dest)]

    exchange(fill_ga, ga_s, ga_r, 1)

    factor = 0.1 * math.log(yarn_factor) + 1.0
    sign = jnp.where(lax.broadcasted_iota(jnp.int32, (1, RB), 1) < HD // 2, -factor, factor)
    for b in range(NB):
        mine = jnp.broadcast_to(seg[b : b + 1, :], (RB, RB)).T
        smaller = jnp.zeros((RB, RB), jnp.int32)
        for other in range(b + 1):
            smaller += jnp.where(seg[other : other + 1, :] < mine, 1, 0)
        first = jnp.sum(smaller, axis=1, keepdims=True)
        start[b] = jnp.broadcast_to(first, (RB, RB))

    def tables(b, carry):
        row = b * RB + lax.broadcasted_iota(jnp.int32, (RB, RB), 0)
        angle = (row - start[b]).astype(F32) * freq[0:1, :]
        cosf[b] = jnp.cos(angle) * factor
        sinf[b] = jnp.sin(angle) * sign
        return carry

    lax.fori_loop(0, NB, tables, 0)

    def find(g, carry):
        source = plan[g] - me * NB
        return tuple(jnp.where(source == j, g // NB, carry[j]) for j in range(NB))

    homes = lax.fori_loop(0, RANKS * NB, find, (jnp.int32(0),) * NB)

    def turned(x, cosine, sine):
        return x * cosine + pltpu.roll(x, HD // 2, 1) * sine

    def pair_copy(src, dst, i):
        return pltpu.make_async_remote_copy(
            src_ref=src, dst_ref=dst, send_sem=pair_send.at[i], recv_sem=pair_recv.at[i],
            device_id={"tensor": partner}, device_id_type=MESH,
        )

    all_moved(kv_s, kv_r, 5).wait_recv()
    is_key = (core == 0).astype(F32)

    def arrive_kv(b, carry):
        origin = plan[me * NB + b] >> 3
        x = kv_r[origin].astype(F32)
        cosine = cosf[b] * is_key + (1.0 - is_key)
        kv2[core, b] = turned(x, cosine, sinf[b] * is_key).astype(BF)
        return carry

    lax.fori_loop(0, NB, arrive_kv, 0)
    share_kv = pair_copy(kv2.at[core], kv2.at[core], 0)
    share_kv.start()

    all_moved(q_s, q_r, 0).wait_recv()
    for b in range(NB):
        block = q_r[plan[me * NB + b] >> 3]
        for h in range(2):
            x = block[:, h * HD : (h + 1) * HD].astype(F32)
            part = pl.ds((b % 2) * RB, RB)
            qs[b // 2 * 2 + h, part] = turned(x, cosf[b], sinf[b]).astype(BF)
    share_kv.wait_recv()

    def key_tile(kb):
        return kv2[0, 2 * kb : 2 * kb + 2].reshape(TILE, HD)

    def value_tile(kb):
        return kv2[1, 2 * kb : 2 * kb + 2].reshape(TILE, HD)

    column = lax.broadcasted_iota(jnp.int32, (TILE, TILE), 1)
    row_of = lax.broadcasted_iota(jnp.int32, (TILE, TILE), 0)
    for t in range(TILES):
        first = start[2 * t : 2 * t + 2].reshape(TILE, RB)
        first = jnp.concatenate([first, first], axis=1)

        def forward(h, carry):
            rows = qs[2 * t + h]
            scores = []
            for kb in range(t + 1):
                raw = dot(rows, key_tile(kb), NT)
                allowed = column + kb * TILE >= first
                if kb == t:
                    allowed = allowed & (column <= row_of)
                scores.append(jnp.where(allowed, raw, masked_score))
            peak = functools.reduce(jnp.maximum, scores)
            peak = jnp.max(peak, axis=1, keepdims=True)
            scores = [jnp.exp2((s - peak) * log2_scale) for s in scores]
            total = jnp.sum(functools.reduce(jnp.add, scores), axis=1, keepdims=True)
            share = 1.0 / total
            out = jnp.zeros((TILE, HD), F32)
            for kb in range(t + 1):
                p = scores[kb] * share
                prob[2 * t + h, :, kb * TILE : (kb + 1) * TILE] = p
                out += dot(p.astype(BF), value_tile(kb), NN)
            outs[2 * t : 2 * t + 2, h] = out.astype(BF).reshape(2, RB, HD)
            return carry

        lax.fori_loop(0, 2, forward, 0)

    def fill_out(buffer, at, dest):
        rows = outs[back_slot(dest)]
        for h in range(2):
            buffer[at, :, h * HD : (h + 1) * HD] = rows[h]

    exchange(fill_out, ao_s, ao_r, 2)

    all_moved(ga_s, ga_r, 1).wait_recv()
    for b in range(NB):
        block = ga_r[plan[me * NB + b] >> 3]
        for h in range(2):
            part = pl.ds((b % 2) * RB, RB)
            gas[b // 2 * 2 + h, part] = block[:, h * HD : (h + 1) * HD]

    dkt[...] = jnp.zeros_like(dkt)
    dvt[...] = jnp.zeros_like(dvt)
    for t in range(TILES):
        cosine = cosf[2 * t : 2 * t + 2].reshape(TILE, HD)
        sine = sinf[2 * t : 2 * t + 2].reshape(TILE, HD)

        def backward(h, carry):
            u = 2 * t + h
            upstream = gas[u]
            rows = qs[u]
            out = outs[2 * t : 2 * t + 2, h].reshape(TILE, HD)
            delta = jnp.sum(
                upstream.astype(F32) * out.astype(F32), axis=1, keepdims=True
            )
            dq = jnp.zeros((TILE, HD), F32)
            for kb in range(t + 1):
                cols = slice(kb * TILE, (kb + 1) * TILE)
                p = prob[u, :, cols]
                dp = dot(upstream, value_tile(kb), NT)
                ds = (p * (dp - delta)).astype(BF)
                dq += dot(ds, key_tile(kb), NN)
                dkt[:, cols] += dot(rows, ds, TN)
                dvt[:, cols] += dot(upstream, p.astype(BF), TN)
            dq = turned(dq * inv_scale, cosine, -sine).astype(BF)
            dq_v[2 * t : 2 * t + 2, h] = dq.reshape(2, RB, HD)
            return carry

        lax.fori_loop(0, 2, backward, 0)

    for b in range(NB):
        cols = slice(b * RB, (b + 1) * RB)
        dk = dkt[:, cols].T * inv_scale
        dkv_own[0, b] = turned(dk, cosf[b], -sinf[b]).astype(BF)
        dkv_own[1, b] = dvt[:, cols].T.astype(BF)
    share_dkv = pair_copy(dkv_own.at[1 - core], dkv_in, 1)
    share_dkv.start()

    def fill_dq(buffer, at, dest):
        rows = dq_v[back_slot(dest)]
        for h in range(2):
            buffer[at, :, h * HD : (h + 1) * HD] = rows[h]

    def fill_dkv(buffer, at, dest):
        buffer[at] = dkv_v[back_slot(dest)]

    share_dkv.wait_recv()
    for b in range(NB):
        dkv_v[b] = (dkv_own[core, b].astype(F32) + dkv_in[b].astype(F32)).astype(BF)
    exchange(fill_dkv, dkv_s, dkv_r, 3, 1)

    all_moved(ao_s, ao_r, 2).wait_recv()
    for j in range(NB):
        aoh[j * RB : (j + 1) * RB] = ao_r[homes[j]]
    chunk = SIDE * WROWS
    for c in range(SIDE):
        rows = g_v[:, :, c * chunk : (c + 1) * chunk].reshape(NB * RB, chunk)
        term = dot(aoh[...], rows, TN).T.astype(BF)
        for e in range(SIDE):
            part = term[e * WROWS : (e + 1) * WROWS]
            w_s[0, c, e] = part[:, :HD]
            w_s[1, e, c] = part[:, HD:]

    mine = (my_x, my_y)

    def beside(axis, by):
        to = lax.rem(mine[axis] + by, SIDE)
        return to, (to * SIDE + my_y if axis == 0 else my_x * SIDE + to)

    def near(kind, half, way):
        to, dest = beside(half, (1, SIDE - 1)[way])
        relayed, plain = pl.ds(2 * way, 2), pl.ds(2 - 2 * way, 2)
        src, dst = (
            (w_s.at[half, lax.rem(mine[half] + 2, SIDE), relayed], w_r.at[half, way]),
            (w_s.at[half, to, plain], wn_r.at[half, way, plain]),
            (wb_s.at[half, way], wn_r.at[half, way, relayed]),
        )[kind]
        return pltpu.make_async_remote_copy(
            src_ref=src, dst_ref=dst,
            send_sem=w_send.at[kind, half, way], recv_sem=w_recv.at[kind, half, way],
            device_id={"dp": dest}, device_id_type=MESH,
        )

    def last(half, o):
        to, dest = beside(1 - half, o)
        return pltpu.make_async_remote_copy(
            src_ref=w2_s.at[half, to], dst_ref=w2_r.at[half, mine[1 - half]],
            send_sem=w2_send.at[half, o - 1], recv_sem=w2_recv.at[half, o - 1],
            device_id={"dp": dest}, device_id_type=MESH,
        )

    ways = [(half, way) for way in range(2) for half in range(2)]
    near_copies = [[near(kind, half, way) for half, way in ways] for kind in range(3)]
    last_copies = [last(half, o) for o in (1, 3, 2) for half in range(2)]
    for copy in near_copies[0]:
        copy.start()
    for copy in near_copies[1]:
        copy.start()
    all_moved(dkv_s, dkv_r, 3).wait_recv()
    for j in range(NB):
        zk[core, zed, j] = dkv_r[homes[j]]
    z_copies = []
    for o in range(1, 4):
        copy = pltpu.make_async_remote_copy(
            src_ref=zk.at[core, zed], dst_ref=zk.at[core, zed],
            send_sem=z_send.at[o - 1], recv_sem=z_recv.at[o - 1],
            device_id={"tensor": lax.rem(zed + o, 4) * 2 + core}, device_id_type=MESH,
        )
        copy.start()
        z_copies.append(copy)

    for i, (half, way) in enumerate(ways):
        to, dest = beside(half, (1, SIDE - 1)[way])
        near_copies[0][i].wait_recv()
        both = w_r[half, way].astype(F32) + w_s[half, to, 2 * way : 2 * way + 2].astype(F32)
        wb_s[half, way] = both.astype(BF)
        near_copies[2][i].start()
    round_of(dq_s, dq_r, 4, 0, 64, fill_dq)

    for copy in near_copies[1] + near_copies[2]:
        copy.wait_recv()
    for half in range(2):
        for e in range(SIDE):
            total = w_s[half, mine[half], e].astype(F32)
            for way in range(2):
                total += wn_r[half, way, e].astype(F32)
            w2_s[half, e] = total.astype(BF)
    for copy in last_copies:
        copy.start()
    for half in range(2):
        w2_r[half, mine[1 - half]] = w2_s[half, mine[1 - half]]
    round_of(dq_s, dq_r, 4, 64, 64, fill_dq)

    for copy in z_copies:
        copy.wait_recv()
    share_z = pair_copy(zk.at[core], zk.at[core], 2)
    share_z.start()
    share_z.wait_recv()
    copies = []
    for k, target in enumerate((gk_hbm, gv_hbm)):
        for z in range(KV):
            copy = pltpu.make_async_copy(
                zk.at[k, z], target.at[:, :, z * HD : (z + 1) * HD], out_sem.at[1 + 4 * k + z]
            )
            copy.start()
            copies.append(copy)

    for copy in last_copies:
        copy.wait_recv()
    for half in range(2):
        total = jnp.zeros((WROWS, HD), F32)
        for r in range(SIDE):
            total += w2_r[half, r].astype(F32)
        gw_v[:, half * HD : (half + 1) * HD] = total * (1.0 / RANKS)
    gw_out = pltpu.make_async_copy(gw_v, gw_hbm, out_sem.at[9])
    gw_out.start()

    all_moved(dq_s, dq_r, 4).wait_recv()
    for j in range(NB):
        q_v[j] = dq_r[homes[j]]
    gq_out = pltpu.make_async_copy(q_v, gq_hbm, out_sem.at[0])
    gq_out.start()

    for kind, (stage, landing) in enumerate(
        ((q_s, q_r), (ga_s, ga_r), (ao_s, ao_r), (dkv_s, dkv_r), (dq_s, dq_r), (kv_s, kv_r))
    ):
        all_moved(stage, landing, kind).wait_send()
    for copy in near_copies[0] + near_copies[1] + near_copies[2] + last_copies:
        copy.wait_send()
    share_kv.wait_send()
    share_dkv.wait_send()
    share_z.wait_send()
    for copy in z_copies:
        copy.wait_send()
    gq_out.wait()
    for copy in copies:
        copy.wait()
    gw_out.wait()


def hand_on(*refs):
    source, target, held, sems = refs[:4], refs[4:8], refs[8:12], refs[12]
    parts = []
    for k in range(4):
        half = source[k].shape[0] // 2
        for h in range(2):
            part = pl.ds(h * half, half)
            sem = sems.at[2 * k + h]
            parts.append(
                (
                    pltpu.make_async_copy(source[k].at[part], held[k].at[part], sem),
                    pltpu.make_async_copy(held[k].at[part], target[k].at[part], sem),
                )
            )
    for load, store in parts:
        load.start()
    for load, store in parts:
        load.wait()
        store.start()
    for load, store in parts:
        store.wait()


def local(query, key, value, grad_out, out_weight, plan, segments):
    blocked = (NB, RB)
    half = yarn_frequencies(HD)
    freq = np.tile(np.concatenate([half, half]), (8, 1)).astype(np.float32)
    hbm = pl.BlockSpec(memory_space=pl.ANY)
    vmem = pl.BlockSpec(memory_space=pltpu.VMEM)
    V = pltpu.VMEM
    dma = pltpu.SemaphoreType.DMA
    rows = NB * RB
    gq, gk, gv, gw = pl.pallas_call(
        kernel,
        out_shape=(
            jax.ShapeDtypeStruct(blocked + (COLS,), BF),
            jax.ShapeDtypeStruct(blocked + (KV * HD,), BF),
            jax.ShapeDtypeStruct(blocked + (KV * HD,), BF),
            jax.ShapeDtypeStruct((WROWS, COLS), F32),
        ),
        in_specs=[pl.BlockSpec(memory_space=pltpu.SMEM), vmem, vmem] + [hbm] * 5,
        out_specs=(hbm,) * 4,
        scratch_shapes=[
            V(blocked + (COLS,), BF),
            V(blocked + (HD,), BF),
            V(blocked + (D,), BF),
            V((D, COLS), BF),
            V((RANKS, RB, COLS), BF),
            V((RANKS, RB, COLS), BF),
            V((RANKS, RB, HD), BF),
            V((RANKS, RB, HD), BF),
            V(blocked + (COLS,), BF),
            V((RANKS, RB, COLS), BF),
            V((RANKS, RB, COLS), BF),
            V((2,) + blocked + (HD,), BF),
            V((2 * TILES, TILE, HD), BF),
            V((2 * TILES, TILE, HD), BF),
            V((NB, 2, RB, HD), BF),
            V((2 * TILES, TILE, rows), F32),
            V((RANKS, RB, COLS), BF),
            V((RANKS, RB, COLS), BF),
            V((NB, 2, RB, HD), BF),
            V((RANKS, RB, COLS), BF),
            V((RANKS, RB, COLS), BF),
            V((HD, rows), F32),
            V((HD, rows), F32),
            V((2,) + blocked + (HD,), BF),
            V(blocked + (HD,), BF),
            V(blocked + (HD,), BF),
            V((RANKS, RB, HD), BF),
            V((RANKS, RB, HD), BF),
            V((2, SIDE, SIDE, WROWS, HD), BF),
            V((2, 2, 2, WROWS, HD), BF),
            V((2, 2, SIDE, WROWS, HD), BF),
            V((2, 2, 2, WROWS, HD), BF),
            V((2, SIDE, WROWS, HD), BF),
            V((2, SIDE, WROWS, HD), BF),
            V((2, KV) + blocked + (HD,), BF),
            V((rows, COLS), BF),
            V((WROWS, COLS), F32),
            V(blocked + (HD,), F32),
            V(blocked + (HD,), F32),
            V(blocked + (RB,), jnp.int32),
            dma((3,)),
            dma((TILES,)),
            dma((6,)),
            dma((6,)),
            dma((3,)),
            dma((3,)),
            dma((3,)),
            dma((3,)),
            dma((3, 2, 2)),
            dma((3, 2, 2)),
            dma((2, 3)),
            dma((2, 3)),
            dma((10,)),
        ],
        compiler_params=pltpu.CompilerParams(
            collective_id=0, has_side_effects=True, vmem_limit_bytes=60 * 2**20
        ),
        cost_estimate=pl.CostEstimate(
            flops=7 * 10**9, bytes_accessed=14 * 2**20, transcendentals=2 * 10**6
        ),
    )(
        plan,
        segments.reshape(NB, RB),
        freq,
        query.reshape(blocked + (COLS,)),
        key.reshape(blocked + (KV * HD,)),
        value.reshape(blocked + (KV * HD,)),
        grad_out.reshape(blocked + (D,)),
        out_weight,
    )
    gq, gk, gv, gw = pl.pallas_call(
        hand_on,
        out_shape=tuple(jax.ShapeDtypeStruct(x.shape, x.dtype) for x in (gq, gk, gv, gw)),
        in_specs=[hbm] * 4,
        out_specs=(hbm,) * 4,
        scratch_shapes=[V(x.shape, x.dtype) for x in (gq, gk, gv, gw)] + [dma((8,))],
    )(gq, gk, gv, gw)
    return (
        gq.reshape(rows, COLS),
        gk.reshape(rows, KV * HD),
        gv.reshape(rows, KV * HD),
        gw,
    )


def solution(mesh):
    in_specs = (
        P("dp", "tensor"),
        P("dp", None),
        P("dp", None),
        P("dp", None),
        P(None, "tensor"),
        P(),
        P("dp"),
    )
    out_specs = (P("dp", "tensor"), P("dp", None), P("dp", None), P("dp", "tensor"))
    return jax.shard_map(local, mesh=mesh, in_specs=in_specs, out_specs=out_specs, check_vma=False)
```
